768 devices in a mesh: col: 24 (over z, core), row: 32 (over y, x).
Axes of the slice: x: 4, y: 8, z: 12, core: 2. Of those that a mesh axis runs over, the one named last changes fastest.
Arguments:
- features: bfloat16 [768, 294912], P('col', 'row'), may hold values from -6 to 6
- adj_values: bfloat16 [2304, 4, 128, 128], P('row'), may hold values from -0.25 to 0.25
- neighbours: int32 [2304, 4], P('row'), may hold values from 0 to 71, as said below
- counts: int32 [2304], P('row'), may hold values from 1 to 4, as said below
- labels: int32 [294912], P('row'), may hold values from 0 to 152
- layer_weight: bfloat16 [768, 1024], replicated, may hold values from -0.21875 to 0.21875
- label_embed: bfloat16 [153, 1024], replicated, may hold values from -6 to 6
Outputs:
- weight_grad: float32 [768, 1024], P('col')
- feature_grad: bfloat16 [768, 294912], P('col', 'row')
The draws below stay inside these ranges and needn't reach their ends.
Inputs may be any that keep to these rules, and one draw needn't show every extreme that they name: `neighbours`: each row holds 4 different block numbers of its own slab, the first being the row block's own number within the slab. `counts`: slots at or past the count are padding and carry no edges.
All inputs are finite; a program needn't handle non-finite values.
Results may differ from the reference program's by a relative error of at most 0.013.
Values may be sent and summed in bfloat16 or wider, within the bound.
A program may use at most 64 MiB of HBM per device.

```python
import math
import jax
import jax.numpy as jnp
from jax import lax

FIN = 768
FOUT = 1024
CLS = 153
BLK = 128
KMAX = 4
SLAB_BLOCKS = 72
NODES = 294912
N_ROW = 32


def draw_neighbours(key, part):
    key = jax.random.fold_in(key, 11)
    row_count = NODES // BLK
    row_keys = jax.random.split(key, row_count)
    shuffled = jax.vmap(lambda row_key: jax.random.permutation(row_key, SLAB_BLOCKS - 1))(row_keys)
    offsets = jnp.concatenate([jnp.zeros((row_count, 1), jnp.int32), 1 + shuffled[:, :KMAX - 1].astype(jnp.int32)], axis=1)
    own_block = jnp.arange(row_count, dtype=jnp.int32) % SLAB_BLOCKS
    return ((own_block[:, None] + offsets) % SLAB_BLOCKS).astype(jnp.int32)


def draw_counts(key, part):
    key = jax.random.fold_in(key, 12)
    row_count = NODES // BLK
    drawn = jax.random.randint(key, (row_count,), 1, KMAX + 1).astype(jnp.int32)
    first_rows = jnp.arange(row_count, dtype=jnp.int32) % SLAB_BLOCKS == 0
    return jnp.where(first_rows, KMAX, drawn).astype(jnp.int32)


def with_ends(result, stream_key, low, top_value):
    shape = result.shape
    spot = [jax.random.randint(jax.random.fold_in(stream_key, axis), (), 0, shape[axis]) for axis in range(len(shape))]
    result = result.at[tuple(spot)].set(low)
    longest = shape.index(max(shape))
    spot[longest] = (spot[longest] + 1) % shape[longest]
    return result.at[tuple(spot)].set(top_value)


def raised(array, stream_key, source, target, blocks, factor):
    owner, partner = [(jnp.arange(array.shape[position]) // (array.shape[position] // blocks)).reshape([-1 if axis == position else 1 for axis in range(array.ndim)]) for position in (source, target)]
    chosen = jax.random.permutation(stream_key, blocks)[partner]
    strong = (owner == chosen) | (owner == (partner + blocks // 2) % blocks)
    return jnp.where(strong, factor * array, array)


def levels(stream_key, dims, cuts, least, high):
    factor_of = 1.0
    for axis_at, parts in cuts:
        steps = jax.random.uniform(jax.random.fold_in(jax.random.fold_in(stream_key, 6), axis_at), (parts,), jnp.float32, least / len(cuts), high / len(cuts))
        factor_of = factor_of * jnp.repeat(jnp.exp(steps), dims[axis_at] // parts).reshape((-1,) + (1,) * (len(dims) - 1 - axis_at))
    return factor_of


def bell_draw(rng, extent, scale, reach, cuts=(), kind=jnp.bfloat16):
    entries = jax.random.normal(rng, extent, jnp.float32) * scale
    if len(cuts) > 0:
        entries = levels(rng, extent, cuts, -0.22, 0.18) * entries
    return jnp.clip(entries, min=-reach, max=reach).astype(kind)


def gaussian_with(key, dims, width, reach, cuts, heavy, kind=jnp.bfloat16):
    values = width * jax.random.normal(key, dims, jnp.float32)
    if cuts:
        values = values * levels(key, dims, cuts, -0.22, 0.18)
    return jnp.clip(raised(values, jax.random.fold_in(key, 3), *heavy), -reach, reach).astype(kind)


def setup_inputs(seed: int = 0) -> dict:
    seeds = jax.random.split(jax.random.key(seed), 8)
    return {
        "features": gaussian_with(seeds[0], (FIN, NODES), 1.0, 6.0, ((0, 24), (1, 32)), (1, 0, 32, 2.75)),
        "adj_values": bell_draw(seeds[1], (NODES // BLK, KMAX, BLK, BLK), (BLK * KMAX) ** -0.5, 0.25, ((0, 32),)),
        "neighbours": draw_neighbours(jax.random.fold_in(seeds[7], 71), 0),
        "counts": draw_counts(jax.random.fold_in(seeds[7], 71), 0),
        "labels": with_ends(jax.random.randint(seeds[4], (NODES,), 0, CLS), jax.random.fold_in(seeds[4], 1), 0, CLS - 1).astype(jnp.int32),
        "layer_weight": bell_draw(seeds[5], (FIN, FOUT), FIN ** -0.5, 0.21875),
        "label_embed": bell_draw(seeds[6], (CLS, FOUT), 1.0, 6.0),
    }


def one_slab(pieces, layer_weight, label_embed):
    slab_features, slab_values, slab_lists, slab_counts, slab_labels = pieces
    live_mask = (jnp.arange(KMAX, dtype=jnp.int32)[None, :] < slab_counts[:, None]).astype(jnp.float32)
    blocks = slab_features.astype(jnp.float32).reshape(FIN, SLAB_BLOCKS, BLK)
    picked = jnp.take(blocks, slab_lists.reshape(-1), axis=1).reshape(FIN, SLAB_BLOCKS, KMAX, BLK)
    picked = picked * live_mask[None, :, :, None]
    values_wide = slab_values.astype(jnp.float32)
    aggregate = jnp.einsum('fiks,iksd->fid', picked, values_wide).reshape(FIN, SLAB_BLOCKS * BLK).astype(jnp.bfloat16)
    hidden = jnp.dot(layer_weight.T, aggregate, preferred_element_type=jnp.float32)
    sigma = jax.nn.sigmoid(hidden)
    derivative = sigma * (1.0 + hidden * (1.0 - sigma))
    one_hot = (slab_labels[None, :] == jnp.arange(CLS, dtype=jnp.int32)[:, None]).astype(jnp.bfloat16)
    target = jnp.dot(label_embed.T, one_hot, preferred_element_type=jnp.float32)
    grad_hidden = (derivative * target).astype(jnp.bfloat16)
    weight_part = jnp.dot(aggregate, grad_hidden.T, preferred_element_type=jnp.float32)
    grad_aggregate = jnp.dot(layer_weight, grad_hidden, preferred_element_type=jnp.float32).astype(jnp.bfloat16)
    grad_blocks = grad_aggregate.astype(jnp.float32).reshape(FIN, SLAB_BLOCKS, BLK)
    contribution = jnp.einsum('fid,iksd->fiks', grad_blocks, values_wide) * live_mask[None, :, :, None]
    feature_part = jnp.zeros((FIN, SLAB_BLOCKS, BLK), jnp.float32).at[:, slab_lists.reshape(-1)].add(contribution.reshape(FIN, SLAB_BLOCKS * KMAX, BLK))
    return (weight_part, feature_part.reshape(FIN, SLAB_BLOCKS * BLK).astype(jnp.bfloat16))

def reference(features, adj_values, neighbours, counts, labels, layer_weight, label_embed):
    slab_nodes = SLAB_BLOCKS * BLK
    stacked = (features.reshape(FIN, N_ROW, slab_nodes).transpose(1, 0, 2), adj_values.reshape(N_ROW, SLAB_BLOCKS, KMAX, BLK, BLK), neighbours.reshape(N_ROW, SLAB_BLOCKS, KMAX), counts.reshape(N_ROW, SLAB_BLOCKS), labels.reshape(N_ROW, slab_nodes))
    weight_parts, feature_parts = lax.map(lambda pieces: one_slab(pieces, layer_weight, label_embed), stacked)
    weight_grad = lax.optimization_barrier(jnp.sum(weight_parts, axis=0)) * (1.0 / math.sqrt(NODES))
    feature_grad = feature_parts.transpose(1, 0, 2).reshape(FIN, NODES)
    return (weight_grad, feature_grad)
```

```python
import functools
import math

import jax
import jax.numpy as jnp
from jax import lax
from jax.experimental import pallas as pl
from jax.experimental.pallas import tpu as pltpu
from jax.sharding import PartitionSpec as P

NX = 4
BF16, F32 = jnp.bfloat16, jnp.float32
MESH = pl.DeviceIdType.MESH
VMEM_LIMIT = 56 * 1024 * 1024


def exchange_kernel(
    col_count,
    row_count,
    factor,
    nbr_ref,
    cnt_ref,
    x_ref,
    lab_ref,
    le_ref,
    adj_hbm,
    w_hbm,
    ret_ref,
    wg_ref,
    x_blocks,
    adj,
    w,
    agg,
    rg,
    gh,
    ga,
    wp,
    core_out,
    core_in,
    x_out,
    x_in,
    q_own,
    y_out,
    y_in,
    z_out,
    z_in,
    y_all,
    x_all,
    adj_sem,
    w_sem,
    own_sem,
    fwd_send,
    fwd_recv,
    bwd_send,
    bwd_recv,
    red_send,
    red_recv,
):
    parts = agg.shape[0]
    fin_dev = x_ref.shape[0]
    fin, fout = w.shape
    slots = nbr_ref.shape[1]
    blk = x_ref.shape[1] // nbr_ref.shape[0]
    ny, nz = row_count // NX, col_count // 2
    rows_x, cols_y = fin_dev // NX, fout // ny
    classes = le_ref.shape[0]

    col, row = lax.axis_index("col"), lax.axis_index("row")
    z, core = col // 2, lax.rem(col, 2)
    y, x = row // NX, lax.rem(row, NX)

    def col_peer(s):
        return lax.rem(col + s, col_count)

    def x_peer(s):
        return y * NX + lax.rem(x + s, NX)

    def y_peer(s):
        return lax.rem(y + s, ny) * NX + x

    barrier = pltpu.get_barrier_semaphore()

    def greet_col(s, c):
        pl.semaphore_signal(barrier, inc=1, device_id={"col": col_peer(s)}, device_id_type=MESH)
        return c

    lax.fori_loop(1, col_count, greet_col, 0)
    for s in range(1, NX):
        pl.semaphore_signal(barrier, inc=1, device_id={"row": x_peer(s)}, device_id_type=MESH)
    for s in range(1, ny):
        pl.semaphore_signal(barrier, inc=1, device_id={"row": y_peer(s)}, device_id_type=MESH)

    pieces = adj_sem.shape[1]
    width = col_count // pieces

    def adj_copy(b, g):
        at = pl.ds(g * width, width)
        return pltpu.make_async_copy(adj_hbm.at[at, b], adj.at[b, at], adj_sem.at[b, g])

    for b in range(parts):
        for g in range(pieces):
            adj_copy(b, g).start()
    w_copy = pltpu.make_async_copy(w_hbm, w, w_sem)
    w_copy.start()

    for k in range(nbr_ref.shape[0]):
        x_blocks[k] = x_ref[:, k * blk : (k + 1) * blk]

    def aggregate(b, g):
        adj_copy(b, g).wait()

        def one(d, c):
            i = d * parts + b
            count = cnt_ref[i]
            picked = []
            for k in range(slots):
                live = jnp.clip(count - k, 0, 1).astype(F32)
                picked.append(x_blocks[nbr_ref[i, k]] * jnp.full((fin_dev, blk), live).astype(BF16))
            total = jnp.dot(
                jnp.concatenate(picked, axis=1), adj[b, d], preferred_element_type=F32
            )
            agg[b, d] = total.astype(BF16)
            return c

        for t in range(width):
            one(g * width + t, 0)

    def send_forward(b):
        def one(s, c):
            d = col_peer(s)
            pltpu.make_async_remote_copy(
                agg.at[b, d],
                rg.at[b, pl.ds(col * fin_dev, fin_dev)],
                fwd_send,
                fwd_recv.at[b],
                device_id={"col": d},
                device_id_type=MESH,
            ).start()
            return c

        lax.fori_loop(1, col_count, one, 0)

    for b in range(parts):
        lax.fori_loop(0, pieces, lambda g, c, b=b: (aggregate(b, g), c)[1], 0)
        if b == 0:
            pl.semaphore_wait(barrier, (col_count - 1) + (NX - 1) + (ny - 1))
        send_forward(b)
        rg[b, pl.ds(pl.multiple_of(col * fin_dev, fin_dev), fin_dev), :] = agg[b, col]

    w_copy.wait()
    tile = min(256, fout)

    def node_part(b, c):
        got = rg.at[b, pl.ds(0, fin - fin_dev)]
        pltpu.make_async_copy(got, got, fwd_recv.at[b]).wait()
        rows = rg[b]
        label = lab_ref[pl.ds(col * parts + b, 1), :]
        one_hot = jnp.where(
            lax.broadcasted_iota(jnp.int32, (classes, blk), 0) == label, 1.0, 0.0
        ).astype(BF16)
        for j in range(fout // tile):
            at = pl.ds(j * tile, tile)
            hidden = lax.dot_general(
                rows, w[:, at], (((0,), (0,)), ((), ())), preferred_element_type=F32
            )
            target = lax.dot_general(
                one_hot, le_ref[:, at], (((0,), (0,)), ((), ())), preferred_element_type=F32
            )
            sigma = 1.0 / (1.0 + jnp.exp(-hidden))
            slope = sigma * (1.0 + hidden * (1.0 - sigma))
            gh[b, :, at] = (slope * target).astype(BF16)
        grad = gh[b]
        step = min(256, fin)
        for m in range(fin // step):
            part = lax.dot_general(
                w[pl.ds(m * step, step), :],
                grad,
                (((1,), (1,)), ((), ())),
                preferred_element_type=F32,
            ).astype(BF16)
            per = step // fin_dev
            ga[b, pl.ds(m * per, per)] = part.reshape(per, fin_dev, blk)

        def send(s, c):
            d = col_peer(s)
            pltpu.make_async_remote_copy(
                ga.at[b, d],
                ret_ref.at[col * parts + b],
                bwd_send,
                bwd_recv,
                device_id={"col": d},
                device_id_type=MESH,
            ).start()
            return c

        lax.fori_loop(1, col_count, send, 0)
        pltpu.make_async_copy(ga.at[b, col], ret_ref.at[col * parts + b], own_sem.at[b]).start()
        return c

    lax.fori_loop(0, parts, node_part, 0)

    left = jnp.concatenate([rg[b] for b in range(parts)], axis=1)

    def weight_part(j, c):
        at = pl.ds(pl.multiple_of(j * tile, tile), tile)
        right = jnp.concatenate([gh[b, :, at] for b in range(parts)], axis=0)
        part = jnp.dot(left, right, preferred_element_type=F32)
        wp[:, :, :, at] = part.reshape(nz, 2, fin_dev, tile)
        return c

    lax.fori_loop(0, fout // tile, weight_part, 0)

    def round_core(i, c):
        core_out[i] = wp[i, 1 - core].astype(BF16)
        return c

    lax.fori_loop(0, nz, round_core, 0)
    to_core = pltpu.make_async_remote_copy(
        core_out,
        core_in,
        red_send.at[0],
        red_recv.at[0],
        device_id={"col": z * 2 + 1 - core},
        device_id_type=MESH,
    )
    to_core.start()
    to_core.wait_recv()

    pair = 16 // rows_x

    def round_x(i, c):
        sums = []
        for t in range(pair):
            total = wp[i * pair + t, core] + core_in[i * pair + t].astype(F32)
            wp[i * pair + t, core] = total
            sums.append(total)
        for k in range(NX):
            piece = jnp.concatenate([v[k * rows_x : (k + 1) * rows_x] for v in sums], axis=0)
            x_out[k, pl.ds(pl.multiple_of(i * 16, 16), 16), :] = piece.astype(BF16)
        return c

    lax.fori_loop(0, nz // pair, round_x, 0)
    for s in range(1, NX):
        pltpu.make_async_remote_copy(
            x_out.at[lax.rem(x + s, NX)],
            x_in.at[s - 1],
            red_send.at[1],
            red_recv.at[1],
            device_id={"row": x_peer(s)},
            device_id_type=MESH,
        ).start()
    pltpu.make_async_copy(x_in, x_in, red_recv.at[1]).wait()

    def round_y(i, c):
        at = pl.ds(pl.multiple_of(i * 16, 16), 16)
        own = pl.ds(pl.multiple_of(x * rows_x, rows_x), rows_x)
        total = jnp.concatenate([wp[i * pair + t, core, own, :] for t in range(pair)], axis=0)
        for s in range(NX - 1):
            total = total + x_in[s, at, :].astype(F32)
        for k in range(ny):
            piece = total[:, k * cols_y : (k + 1) * cols_y]
            q_own[k, at, :] = piece
            y_out[k, at, :] = piece.astype(BF16)
        return c

    lax.fori_loop(0, nz // pair, round_y, 0)

    def send_y(s, c):
        pltpu.make_async_remote_copy(
            y_out.at[lax.rem(y + s, ny)],
            y_in.at[s - 1],
            red_send.at[2],
            red_recv.at[2],
            device_id={"row": y_peer(s)},
            device_id_type=MESH,
        ).start()
        return c

    lax.fori_loop(1, ny, send_y, 0)
    pltpu.make_async_copy(y_in, y_in, red_recv.at[2]).wait()

    total = q_own[y]
    for s in range(ny - 1):
        total = total + y_in[s].astype(F32)
    z_out[...] = total.reshape(nz, rows_x, cols_y)

    def send_z(s, c):
        other = lax.rem(z + s, nz)
        pltpu.make_async_remote_copy(
            z_out.at[other],
            z_in.at[s - 1],
            red_send.at[3],
            red_recv.at[3],
            device_id={"col": other * 2 + core},
            device_id_type=MESH,
        ).start()
        return c

    lax.fori_loop(1, nz, send_z, 0)
    pltpu.make_async_copy(z_in, z_in, red_recv.at[3]).wait()
    total = z_out[z]
    for s in range(nz - 1):
        total = total + z_in[s]
    y_all[y] = total * factor

    def share_y(s, c):
        pltpu.make_async_remote_copy(
            y_all.at[y],
            y_all.at[y],
            red_send.at[4],
            red_recv.at[4],
            device_id={"row": y_peer(s)},
            device_id_type=MESH,
        ).start()
        return c

    lax.fori_loop(1, ny, share_y, 0)
    got = y_all.at[pl.ds(0, ny - 1)]
    pltpu.make_async_copy(got, got, red_recv.at[4]).wait()
    x_all[x] = jnp.concatenate([y_all[k] for k in range(ny)], axis=1)
    for s in range(1, NX):
        pltpu.make_async_remote_copy(
            x_all.at[x],
            x_all.at[x],
            red_send.at[5],
            red_recv.at[5],
            device_id={"row": x_peer(s)},
            device_id_type=MESH,
        ).start()
    got = x_all.at[pl.ds(0, NX - 1)]
    pltpu.make_async_copy(got, got, red_recv.at[5]).wait()
    wg_ref[...] = x_all[...].reshape(fin_dev, fout)

    got = ret_ref.at[pl.ds(0, (col_count - 1) * parts)]
    pltpu.make_async_copy(got, got, bwd_recv).wait()
    for b in range(parts):
        pltpu.make_async_copy(ga.at[b, col], ret_ref.at[col * parts + b], own_sem.at[b]).wait()
    sent = agg.at[:, pl.ds(0, col_count - 1)]
    pltpu.make_async_copy(sent, sent, fwd_send).wait()
    sent = ga.at[:, pl.ds(0, col_count - 1)]
    pltpu.make_async_copy(sent, sent, bwd_send).wait()
    to_core.wait_send()
    pltpu.make_async_copy(x_in, x_in, red_send.at[1]).wait()
    pltpu.make_async_copy(y_in, y_in, red_send.at[2]).wait()
    pltpu.make_async_copy(z_in, z_in, red_send.at[3]).wait()
    sent = y_all.at[pl.ds(0, ny - 1)]
    pltpu.make_async_copy(sent, sent, red_send.at[4]).wait()
    sent = x_all.at[pl.ds(0, NX - 1)]
    pltpu.make_async_copy(sent, sent, red_send.at[5]).wait()


def spread_kernel(nbr_ref, cnt_ref, ga_ref, adj_hbm, out_ref, adj, acc, adj_sem):
    blocks, slots = nbr_ref.shape
    fin_dev, blk = ga_ref.shape[1:]
    pieces = adj_sem.shape[0]
    width = blocks // pieces

    def adj_copy(g):
        at = pl.ds(g * width, width)
        return pltpu.make_async_copy(adj_hbm.at[at], adj.at[at], adj_sem.at[g])

    for g in range(pieces):
        adj_copy(g).start()
    acc[...] = jnp.zeros_like(acc)

    def piece(g, c):
        adj_copy(g).wait()
        terms = []
        for t in range(width):
            i = g * width + t
            terms.append(
                lax.dot_general(
                    ga_ref[i], adj[i], (((1,), (1,)), ((), ())), preferred_element_type=F32
                )
            )
        for t in range(width):
            i = g * width + t
            count = cnt_ref[i]
            for k in range(slots):
                term = terms[t][:, k * blk : (k + 1) * blk]
                at = nbr_ref[i, k]
                acc[at] = acc[at] + jnp.where(k < count, term, jnp.zeros_like(term))
        return c

    lax.fori_loop(0, pieces, piece, 0)
    for b in range(blocks):
        out_ref[:, b * blk : (b + 1) * blk] = acc[b].astype(BF16)


def shards(features, adj_values, neighbours, counts, labels, layer_weight, label_embed):
    fin_dev, slab_nodes = features.shape
    blocks, slots, blk, _ = adj_values.shape
    fin, fout = layer_weight.shape
    col_count, row_count = lax.axis_size("col"), lax.axis_size("row")
    ny, nz = row_count // NX, col_count // 2
    rows_x, cols_y = fin_dev // NX, fout // ny
    parts = blocks // col_count
    factor = 1.0 / math.sqrt(slab_nodes * row_count)
    in_vmem = pl.BlockSpec(memory_space=pltpu.VMEM)
    in_smem = pl.BlockSpec(memory_space=pltpu.SMEM)
    anywhere = pl.BlockSpec(memory_space=pl.ANY)
    pieces = 4
    dma = pltpu.SemaphoreType.DMA

    returned, weight_grad = pl.pallas_call(
        functools.partial(exchange_kernel, col_count, row_count, factor),
        out_shape=(
            jax.ShapeDtypeStruct((blocks, fin_dev, blk), BF16),
            jax.ShapeDtypeStruct((fin_dev, fout), F32),
        ),
        in_specs=[in_smem, in_smem, in_vmem, in_vmem, in_vmem, anywhere, anywhere],
        out_specs=(anywhere, in_vmem),
        scratch_shapes=[
            pltpu.VMEM((blocks, fin_dev, blk), BF16),
            pltpu.VMEM((parts, col_count, slots * blk, blk), BF16),
            pltpu.VMEM((fin, fout), BF16),
            pltpu.VMEM((parts, col_count, fin_dev, blk), BF16),
            pltpu.VMEM((parts, fin, blk), BF16),
            pltpu.VMEM((parts, blk, fout), BF16),
            pltpu.VMEM((parts, col_count, fin_dev, blk), BF16),
            pltpu.VMEM((nz, 2, fin_dev, fout), F32),
            pltpu.VMEM((nz, fin_dev, fout), BF16),
            pltpu.VMEM((nz, fin_dev, fout), BF16),
            pltpu.VMEM((NX, nz * rows_x, fout), BF16),
            pltpu.VMEM((NX - 1, nz * rows_x, fout), BF16),
            pltpu.VMEM((ny, nz * rows_x, cols_y), F32),
            pltpu.VMEM((ny, nz * rows_x, cols_y), BF16),
            pltpu.VMEM((ny - 1, nz * rows_x, cols_y), BF16),
            pltpu.VMEM((nz, rows_x, cols_y), F32),
            pltpu.VMEM((nz - 1, rows_x, cols_y), F32),
            pltpu.VMEM((ny, rows_x, cols_y), F32),
            pltpu.VMEM((NX, rows_x, fout), F32),
            dma((parts, pieces)),
            dma,
            dma((parts,)),
            dma,
            dma((parts,)),
            dma,
            dma,
            dma((6,)),
            dma((6,)),
        ],
        compiler_params=pltpu.CompilerParams(
            collective_id=0, has_side_effects=True, vmem_limit_bytes=VMEM_LIMIT
        ),
        name="exchange",
    )(
        neighbours,
        counts,
        features,
        labels.reshape(blocks, blk),
        label_embed,
        adj_values.reshape(col_count, parts, slots * blk, blk),
        layer_weight,
    )

    spread_pieces = 12
    feature_grad = pl.pallas_call(
        spread_kernel,
        out_shape=jax.ShapeDtypeStruct((fin_dev, slab_nodes), BF16),
        in_specs=[in_smem, in_smem, in_vmem, anywhere],
        out_specs=in_vmem,
        scratch_shapes=[
            pltpu.VMEM((blocks, slots * blk, blk), BF16),
            pltpu.VMEM((blocks, fin_dev, blk), F32),
            dma((spread_pieces,)),
        ],
        compiler_params=pltpu.CompilerParams(vmem_limit_bytes=VMEM_LIMIT),
        name="spread",
    )(neighbours, counts, returned, adj_values.reshape(blocks, slots * blk, blk))
    return weight_grad, feature_grad


def solution(mesh):
    return jax.shard_map(
        shards,
        mesh=mesh,
        in_specs=(
            P("col", "row"),
            P("row", None, None, None),
            P("row", None),
            P("row"),
            P("row"),
            P(),
            P(),
        ),
        out_specs=(P("col", None), P("col", "row")),
        check_vma=False,
    )
```

```python
import functools
import math

import jax
import jax.numpy as jnp
from jax import lax
from jax.experimental import pallas as pl
from jax.experimental.pallas import tpu as pltpu
from jax.sharding import PartitionSpec as P

NX = 4
BF16, F32 = jnp.bfloat16, jnp.float32
MESH = pl.DeviceIdType.MESH
VMEM_LIMIT = 56 * 1024 * 1024


def exchange_kernel(
    col_count,
    row_count,
    factor,
    nbr_ref,
    cnt_ref,
    nbr_rows,
    cnt_row,
    x_ref,
    lab_ref,
    le_ref,
    adj_hbm,
    w_hbm,
    wg_ref,
    fg_ref,
    x_blocks,
    adj,
    w,
    agg,
    rg,
    gh,
    ga,
    ret,
    one_hots,
    terms,
    total_f,
    wp,
    core_out,
    core_in,
    x_out,
    x_in,
    q_own,
    y_out,
    y_in,
    z_out,
    z_in,
    y_all,
    x_all,
    adj_sem,
    w_sem,
    fwd_send,
    fwd_recv,
    bwd_send,
    bwd_recv,
    red_send,
    red_recv,
    last_send,
    last_recv,
):
    parts = agg.shape[0]
    fin_dev = x_ref.shape[0]
    fin, fout = w.shape
    slots = nbr_ref.shape[0]
    blocks = nbr_ref.shape[1]
    blk = x_ref.shape[1] // blocks
    ny, nz = row_count // NX, col_count // 2
    rows_x, cols_y = fin_dev // NX, fout // ny
    classes = le_ref.shape[0]

    col, row = lax.axis_index("col"), lax.axis_index("row")
    z, core = col // 2, lax.rem(col, 2)
    y, x = row // NX, lax.rem(row, NX)

    def col_peer(s):
        return lax.rem(col + s, col_count)

    def x_peer(s):
        return y * NX + lax.rem(x + s, NX)

    def y_peer(s):
        return lax.rem(y + s, ny) * NX + x

    barrier = pltpu.get_barrier_semaphore()

    def greet_col(s, c):
        pl.semaphore_signal(barrier, inc=1, device_id={"col": col_peer(s)}, device_id_type=MESH)
        return c

    lax.fori_loop(1, col_count, greet_col, 0)
    for s in range(1, NX):
        pl.semaphore_signal(barrier, inc=1, device_id={"row": x_peer(s)}, device_id_type=MESH)
    for s in range(1, ny):
        pl.semaphore_signal(barrier, inc=1, device_id={"row": y_peer(s)}, device_id_type=MESH)

    pieces = adj_sem.shape[1]
    width = col_count // pieces

    def adj_copy(b, g):
        at = pl.ds(g * width, width)
        return pltpu.make_async_copy(adj_hbm.at[b, at], adj.at[b, at], adj_sem.at[b, g])

    for b in range(parts):
        for g in range(pieces):
            adj_copy(b, g).start()
    w_copy = pltpu.make_async_copy(w_hbm, w, w_sem)
    w_copy.start()

    for k in range(blocks):
        x_blocks[k] = x_ref[:, k * blk : (k + 1) * blk]

    def aggregate(b, g):
        adj_copy(b, g).wait()

        def one(d, c):
            i = b * col_count + d
            count = cnt_ref[i]
            picked = []
            for k in range(slots):
                live = jnp.clip(count - k, 0, 1).astype(F32)
                picked.append(x_blocks[nbr_ref[k, i]] * jnp.full((fin_dev, blk), live).astype(BF16))
            total = jnp.dot(
                jnp.concatenate(picked, axis=1), adj[b, d], preferred_element_type=F32
            )
            agg[b, d] = total.astype(BF16)
            return c

        for t in range(width):
            one(g * width + t, 0)

    def send_forward(b):
        def one(s, c):
            d = col_peer(s)
            pltpu.make_async_remote_copy(
                agg.at[b, d],
                rg.at[b, pl.ds(col * fin_dev, fin_dev)],
                fwd_send,
                fwd_recv.at[b],
                device_id={"col": d},
                device_id_type=MESH,
            ).start()
            return c

        lax.fori_loop(1, col_count, one, 0)

    for b in range(parts):
        lax.fori_loop(0, pieces, lambda g, c, b=b: (aggregate(b, g), c)[1], 0)
        if b == 0:
            pl.semaphore_wait(barrier, (col_count - 1) + (NX - 1) + (ny - 1))
        send_forward(b)
        rg[b, pl.ds(pl.multiple_of(col * fin_dev, fin_dev), fin_dev), :] = agg[b, col]

    square = (blocks, blocks)
    diagonal = lax.broadcasted_iota(jnp.int32, square, 0) == lax.broadcasted_iota(jnp.int32, square, 1)
    goes_to = []
    for k in range(slots):
        line = jnp.where(cnt_row[...] > k, nbr_rows[k : k + 1, :] + 1, 0).astype(F32)
        goes_to.append(jnp.sum(jnp.where(diagonal, line, 0.0), axis=1, keepdims=True))
    for b in range(parts):
        wide = (blocks, one_hots.shape[2])
        source = lax.broadcasted_iota(jnp.int32, wide, 0)
        lane = lax.broadcasted_iota(jnp.int32, wide, 1)
        line = jnp.zeros((1, wide[1]), F32)
        for h in range(2):
            for k in range(slots):
                low = (h * slots + k) * col_count
                here = (source - b * col_count == lane - low) & (lane >= low)
                here = here & (lane < low + col_count)
                line = line + jnp.sum(jnp.where(here, goes_to[k], 0.0), axis=0, keepdims=True)
        target = lax.broadcasted_iota(jnp.int32, one_hots.shape[1:], 0).astype(F32) + 1.0
        one_hots[b] = jnp.where(target == line, 1.0, 0.0).astype(BF16)

    w_copy.wait()
    tile = min(256, fout)

    def node_part(b, c):
        got = rg.at[b, pl.ds(0, fin - fin_dev)]
        pltpu.make_async_copy(got, got, fwd_recv.at[b]).wait()
        rows = rg[b]
        label = lab_ref[pl.ds(b * col_count + col, 1), :]
        one_hot = jnp.where(
            lax.broadcasted_iota(jnp.int32, (classes, blk), 0) == label, 1.0, 0.0
        ).astype(BF16)
        for j in range(fout // tile):
            at = pl.ds(j * tile, tile)
            hidden = lax.dot_general(
                rows, w[:, at], (((0,), (0,)), ((), ())), preferred_element_type=F32
            )
            target = lax.dot_general(
                one_hot, le_ref[:, at], (((0,), (0,)), ((), ())), preferred_element_type=F32
            )
            sigma = 1.0 / (1.0 + jnp.exp(-hidden))
            slope = sigma * (1.0 + hidden * (1.0 - sigma))
            gh[b, :, at] = (slope * target).astype(BF16)
        grad = gh[b]
        step = min(256, fin)
        for m in range(fin // step):
            part = lax.dot_general(
                w[pl.ds(m * step, step), :],
                grad,
                (((1,), (1,)), ((), ())),
                preferred_element_type=F32,
            ).astype(BF16)
            per = step // fin_dev
            ga[b, pl.ds(m * per, per)] = part.reshape(per, fin_dev, blk)

        def send(s, c):
            d = col_peer(s)
            pltpu.make_async_remote_copy(
                ga.at[b, d],
                ret.at[b, col],
                bwd_send,
                bwd_recv.at[b],
                device_id={"col": d},
                device_id_type=MESH,
            ).start()
            return c

        lax.fori_loop(1, col_count, send, 0)
        ret[b, col] = ga[b, col]
        return c

    lax.fori_loop(0, parts, node_part, 0)

    entries = slots * col_count
    f_rows = total_f.shape[0] // fin_dev

    def spread(b):
        got = ret.at[b, pl.ds(0, col_count - 1)]
        pltpu.make_async_copy(got, got, bwd_recv.at[b]).wait()
        group = 4

        def make(g, c):
            for t in range(group):
                d = g * group + t
                term = lax.dot_general(
                    ret[b, d], adj[b, d], (((1,), (1,)), ((), ())), preferred_element_type=F32
                )
                for k in range(slots):
                    at = pl.multiple_of((k * col_count + d) * fin_dev, fin_dev)
                    terms[pl.ds(at, fin_dev), :] = term[:, k * blk : (k + 1) * blk]
            return c

        lax.fori_loop(0, col_count // group, make, 0)
        table = one_hots[b]

        def add(p, c):
            for t in range(2):
                f = (p * 2 + t) * 2
                term = jnp.concatenate(
                    [terms[pl.ds(f + h, entries, stride=fin_dev), :] for h in range(2)], axis=1
                )
                high = term.astype(BF16)
                low = (term - high.astype(F32)).astype(BF16)
                part = jnp.dot(
                    table, jnp.concatenate([high, low], axis=0), preferred_element_type=F32
                )
                for h in range(2):
                    at = pl.ds(pl.multiple_of((f + h) * f_rows, 8), f_rows)
                    piece = part[:, h * blk : (h + 1) * blk]
                    total_f[at, :] = piece if b == 0 else total_f[at, :] + piece
            return c

        lax.fori_loop(0, fin_dev // 4, add, 0)

    chunks, zc = core_out.shape[0], core_out.shape[1]
    pair = 16 // rows_x
    rows_c = zc * 2 * fin_dev

    def weight_part(g):
        at = pl.ds(g * rows_c, rows_c)
        left = jnp.concatenate([rg[b, at, :] for b in range(parts)], axis=1)

        def columns(j, c):
            at = pl.ds(pl.multiple_of(j * tile, tile), tile)
            right = jnp.concatenate([gh[b, :, at] for b in range(parts)], axis=0)
            part = jnp.dot(left, right, preferred_element_type=F32)
            wp[g, :, :, :, at] = part.reshape(zc, 2, fin_dev, tile)
            return c

        lax.fori_loop(0, fout // tile, columns, 0)

        def round_core(i, c):
            core_out[g, i] = wp[g, i, 1 - core].astype(BF16)
            return c

        lax.fori_loop(0, zc, round_core, 0)

    def to_core(g):
        return pltpu.make_async_remote_copy(
            core_out.at[g],
            core_in.at[g],
            red_send.at[0, g],
            red_recv.at[0, g],
            device_id={"col": z * 2 + 1 - core},
            device_id_type=MESH,
        )

    def send_x(g):
        to_core(g).wait_recv()

        def round_x(i, c):
            sums = []
            for t in range(pair):
                total = wp[g, i * pair + t, core] + core_in[g, i * pair + t].astype(F32)
                wp[g, i * pair + t, core] = total
                sums.append(total)
            for k in range(NX):
                piece = jnp.concatenate([v[k * rows_x : (k + 1) * rows_x] for v in sums], axis=0)
                x_out[g, k, pl.ds(pl.multiple_of(i * 16, 16), 16), :] = piece.astype(BF16)
            return c

        lax.fori_loop(0, zc // pair, round_x, 0)
        for s in range(1, NX):
            pltpu.make_async_remote_copy(
                x_out.at[g, lax.rem(x + s, NX)],
                x_in.at[g, s - 1],
                red_send.at[1, g],
                red_recv.at[1, g],
                device_id={"row": x_peer(s)},
                device_id_type=MESH,
            ).start()

    def send_y(g):
        pltpu.make_async_copy(x_in.at[g], x_in.at[g], red_recv.at[1, g]).wait()

        def round_y(i, c):
            at = pl.ds(pl.multiple_of(i * 16, 16), 16)
            own = pl.ds(pl.multiple_of(x * rows_x, rows_x), rows_x)
            total = jnp.concatenate(
                [wp[g, i * pair + t, core, own, :] for t in range(pair)], axis=0
            )
            for s in range(NX - 1):
                total = total + x_in[g, s, at, :].astype(F32)
            for k in range(ny):
                piece = total[:, k * cols_y : (k + 1) * cols_y]
                q_own[g, k, at, :] = piece
                y_out[g, k, at, :] = piece.astype(BF16)
            return c

        lax.fori_loop(0, zc // pair, round_y, 0)

        def one(s, c):
            pltpu.make_async_remote_copy(
                y_out.at[g, lax.rem(y + s, ny)],
                y_in.at[g, s - 1],
                red_send.at[2, g],
                red_recv.at[2, g],
                device_id={"row": y_peer(s)},
                device_id_type=MESH,
            ).start()
            return c

        lax.fori_loop(1, ny, one, 0)

    for g in range(chunks):
        weight_part(g)
        to_core(g).start()
        if g > 0:
            send_x(g - 1)
    send_x(chunks - 1)
    spread(0)
    for g in range(chunks):
        send_y(g)

    for g in range(chunks):
        pltpu.make_async_copy(y_in.at[g], y_in.at[g], red_recv.at[2, g]).wait()
        total = q_own[g, y]
        for s in range(ny - 1):
            total = total + y_in[g, s].astype(F32)
        z_out[g * zc : (g + 1) * zc] = total.reshape(zc, rows_x, cols_y)

    def send_z(s, c):
        other = lax.rem(z + s, nz)
        pltpu.make_async_remote_copy(
            z_out.at[other],
            z_in.at[s - 1],
            last_send.at[0],
            last_recv.at[0],
            device_id={"col": other * 2 + core},
            device_id_type=MESH,
        ).start()
        return c

    lax.fori_loop(1, nz, send_z, 0)
    for b in range(1, parts - 1):
        spread(b)
    pltpu.make_async_copy(z_in, z_in, last_recv.at[0]).wait()
    total = z_out[z]
    for s in range(nz - 1):
        total = total + z_in[s]
    y_all[y] = total * factor

    def share_y(s, c):
        pltpu.make_async_remote_copy(
            y_all.at[y],
            y_all.at[y],
            last_send.at[1],
            last_recv.at[1],
            device_id={"row": y_peer(s)},
            device_id_type=MESH,
        ).start()
        return c

    lax.fori_loop(1, ny, share_y, 0)
    spread(parts - 1)
    got = y_all.at[pl.ds(0, ny - 1)]
    pltpu.make_async_copy(got, got, last_recv.at[1]).wait()
    x_all[x] = jnp.concatenate([y_all[k] for k in range(ny)], axis=1)
    for s in range(1, NX):
        pltpu.make_async_remote_copy(
            x_all.at[x],
            x_all.at[x],
            last_send.at[2],
            last_recv.at[2],
            device_id={"row": x_peer(s)},
            device_id_type=MESH,
        ).start()
    for k in range(blocks):
        grad = total_f[pl.ds(k, fin_dev, stride=f_rows), :]
        fg_ref[:, k * blk : (k + 1) * blk] = grad.astype(BF16)
    got = x_all.at[pl.ds(0, NX - 1)]
    pltpu.make_async_copy(got, got, last_recv.at[2]).wait()
    wg_ref[...] = x_all[...].reshape(fin_dev, fout)

    sent = agg.at[:, pl.ds(0, col_count - 1)]
    pltpu.make_async_copy(sent, sent, fwd_send).wait()
    sent = ga.at[:, pl.ds(0, col_count - 1)]
    pltpu.make_async_copy(sent, sent, bwd_send).wait()
    for g in range(chunks):
        to_core(g).wait_send()
        pltpu.make_async_copy(x_in.at[g], x_in.at[g], red_send.at[1, g]).wait()
        pltpu.make_async_copy(y_in.at[g], y_in.at[g], red_send.at[2, g]).wait()
    pltpu.make_async_copy(z_in, z_in, last_send.at[0]).wait()
    sent = y_all.at[pl.ds(0, ny - 1)]
    pltpu.make_async_copy(sent, sent, last_send.at[1]).wait()
    sent = x_all.at[pl.ds(0, NX - 1)]
    pltpu.make_async_copy(sent, sent, last_send.at[2]).wait()


def shards(features, adj_values, neighbours, counts, labels, layer_weight, label_embed):
    fin_dev, slab_nodes = features.shape
    blocks, slots, blk, _ = adj_values.shape
    fin, fout = layer_weight.shape
    col_count, row_count = lax.axis_size("col"), lax.axis_size("row")
    ny, nz = row_count // NX, col_count // 2
    rows_x, cols_y = fin_dev // NX, fout // ny
    parts = blocks // col_count
    factor = 1.0 / math.sqrt(slab_nodes * row_count)
    in_vmem = pl.BlockSpec(memory_space=pltpu.VMEM)
    in_smem = pl.BlockSpec(memory_space=pltpu.SMEM)
    anywhere = pl.BlockSpec(memory_space=pl.ANY)
    pieces = 4
    zc = 4 if nz % 4 == 0 and nz > 4 else 2
    chunks = nz // zc
    rows_c = zc * rows_x
    f_rows = -(-blocks // 16) * 16
    dma = pltpu.SemaphoreType.DMA

    return pl.pallas_call(
        functools.partial(exchange_kernel, col_count, row_count, factor),
        out_shape=(
            jax.ShapeDtypeStruct((fin_dev, fout), F32),
            jax.ShapeDtypeStruct((fin_dev, slab_nodes), BF16),
        ),
        in_specs=[in_smem] * 2 + [in_vmem] * 5 + [anywhere] * 2,
        out_specs=(in_vmem, in_vmem),
        scratch_shapes=[
            pltpu.VMEM((blocks, fin_dev, blk), BF16),
            pltpu.VMEM((parts, col_count, slots * blk, blk), BF16),
            pltpu.VMEM((fin, fout), BF16),
            pltpu.VMEM((parts, col_count, fin_dev, blk), BF16),
            pltpu.VMEM((parts, fin, blk), BF16),
            pltpu.VMEM((parts, blk, fout), BF16),
            pltpu.VMEM((parts, col_count, fin_dev, blk), BF16),
            pltpu.VMEM((parts, col_count, fin_dev, blk), BF16),
            pltpu.VMEM((parts, f_rows, 2 * slots * col_count), BF16),
            pltpu.VMEM((slots * col_count * fin_dev, blk), F32),
            pltpu.VMEM((fin_dev * f_rows, blk), F32),
            pltpu.VMEM((chunks, zc, 2, fin_dev, fout), F32),
            pltpu.VMEM((chunks, zc, fin_dev, fout), BF16),
            pltpu.VMEM((chunks, zc, fin_dev, fout), BF16),
            pltpu.VMEM((chunks, NX, rows_c, fout), BF16),
            pltpu.VMEM((chunks, NX - 1, rows_c, fout), BF16),
            pltpu.VMEM((chunks, ny, rows_c, cols_y), F32),
            pltpu.VMEM((chunks, ny, rows_c, cols_y), BF16),
            pltpu.VMEM((chunks, ny - 1, rows_c, cols_y), BF16),
            pltpu.VMEM((nz, rows_x, cols_y), F32),
            pltpu.VMEM((nz - 1, rows_x, cols_y), F32),
            pltpu.VMEM((ny, rows_x, cols_y), F32),
            pltpu.VMEM((NX, rows_x, fout), F32),
            dma((parts, pieces)),
            dma,
            dma,
            dma((parts,)),
            dma,
            dma((parts,)),
            dma((3, chunks)),
            dma((3, chunks)),
            dma((3,)),
            dma((3,)),
        ],
        compiler_params=pltpu.CompilerParams(
            collective_id=0, has_side_effects=True, vmem_limit_bytes=VMEM_LIMIT
        ),
        name="exchange",
    )(
        neighbours.T,
        counts,
        neighbours.T,
        counts.reshape(1, blocks),
        features,
        labels.reshape(blocks, blk),
        label_embed,
        adj_values.reshape(parts, col_count, slots * blk, blk),
        layer_weight,
    )


def solution(mesh):
    return jax.shard_map(
        shards,
        mesh=mesh,
        in_specs=(
            P("col", "row"),
            P("row", None, None, None),
            P("row", None),
            P("row"),
            P("row"),
            P(),
            P(),
        ),
        out_specs=(P("col", None), P("col", "row")),
        check_vma=False,
    )
```

```python
import functools
import math

import jax
import jax.numpy as jnp
from jax import lax
from jax.experimental import pallas as pl
from jax.experimental.pallas import tpu as pltpu
from jax.sharding import PartitionSpec as P

NX = 4
BF16, F32 = jnp.bfloat16, jnp.float32
MESH = pl.DeviceIdType.MESH
VMEM_LIMIT = 56 * 1024 * 1024


def exchange_kernel(
    col_count,
    row_count,
    factor,
    nbr_ref,
    cnt_ref,
    nbr_rows,
    cnt_row,
    x_ref,
    lab_ref,
    le_ref,
    adj_hbm,
    w_hbm,
    wg_ref,
    fg_ref,
    x_blocks,
    adj,
    w,
    agg,
    rg,
    gh,
    ga,
    ret,
    one_hots,
    terms,
    total_f,
    wp,
    core_out,
    core_in,
    x_out,
    x_in,
    q_own,
    y_out,
    y_in,
    z_out,
    z_in,
    shared,
    adj_sem,
    w_sem,
    fwd_send,
    fwd_recv,
    bwd_send,
    bwd_recv,
    red_send,
    red_recv,
    last_send,
    last_recv,
):
    parts = agg.shape[0]
    fin_dev = x_ref.shape[0]
    fin, fout = w.shape
    slots = nbr_ref.shape[0]
    blocks = nbr_ref.shape[1]
    blk = x_ref.shape[1] // blocks
    ny, nz = row_count // NX, col_count // 2
    rows_x, cols_y = fin_dev // NX, fout // ny
    classes = le_ref.shape[0]

    col, row = lax.axis_index("col"), lax.axis_index("row")
    z, core = col // 2, lax.rem(col, 2)
    y, x = row // NX, lax.rem(row, NX)

    def col_peer(s):
        return lax.rem(col + s, col_count)

    def x_peer(s):
        return y * NX + lax.rem(x + s, NX)

    def row_peer(s):
        return lax.rem(row + s, row_count)

    def y_peer(s):
        return lax.rem(y + s, ny) * NX + x

    barrier = pltpu.get_barrier_semaphore()

    def greet_col(s, c):
        pl.semaphore_signal(barrier, inc=1, device_id={"col": col_peer(s)}, device_id_type=MESH)
        return c

    lax.fori_loop(1, col_count, greet_col, 0)
    def greet_row(s, c):
        pl.semaphore_signal(barrier, inc=1, device_id={"row": row_peer(s)}, device_id_type=MESH)
        return c

    lax.fori_loop(1, row_count, greet_row, 0)

    pieces = adj_sem.shape[1]
    width = col_count // pieces

    def adj_copy(b, g):
        at = pl.ds(g * width, width)
        return pltpu.make_async_copy(adj_hbm.at[b, at], adj.at[b, at], adj_sem.at[b, g])

    def group(g):
        return lax.rem(col // width + g, pieces)

    for b in range(parts):
        for g in range(pieces):
            adj_copy(b, group(g)).start()
    w_copy = pltpu.make_async_copy(w_hbm, w, w_sem)
    w_copy.start()

    for k in range(blocks):
        x_blocks[k] = x_ref[:, k * blk : (k + 1) * blk]

    def aggregate(b, g):
        adj_copy(b, g).wait()

        def one(d, c):
            i = b * col_count + d
            count = cnt_ref[i]
            picked = []
            for k in range(slots):
                live = jnp.clip(count - k, 0, 1).astype(F32)
                picked.append(x_blocks[nbr_ref[k, i]] * jnp.full((fin_dev, blk), live).astype(BF16))
            total = jnp.dot(
                jnp.concatenate(picked, axis=1), adj[b, d], preferred_element_type=F32
            )
            agg[b, d] = total.astype(BF16)
            return c

        for t in range(width):
            one(g * width + t, 0)

    def send_forward(b, g):
        def one(t, c):
            d = g * width + lax.rem(col + t, width)

            @pl.when(d != col)
            def _():
                pltpu.make_async_remote_copy(
                    agg.at[b, d],
                    rg.at[b, pl.ds(col * fin_dev, fin_dev)],
                    fwd_send,
                    fwd_recv.at[b],
                    device_id={"col": d},
                    device_id_type=MESH,
                ).start()

            return c

        lax.fori_loop(0, width, one, 0)

    aggregate(0, group(0))
    pl.semaphore_wait(barrier, (col_count - 1) + (row_count - 1))
    send_forward(0, group(0))
    for b in range(parts):

        def both(g, c, b=b):
            aggregate(b, group(g))
            send_forward(b, group(g))
            return c

        lax.fori_loop(1 if b == 0 else 0, pieces, both, 0)
        rg[b, pl.ds(pl.multiple_of(col * fin_dev, fin_dev), fin_dev), :] = agg[b, col]

    square = (blocks, blocks)
    diagonal = lax.broadcasted_iota(jnp.int32, square, 0) == lax.broadcasted_iota(jnp.int32, square, 1)
    goes_to = []
    for k in range(slots):
        line = jnp.where(cnt_row[...] > k, nbr_rows[k : k + 1, :] + 1, 0).astype(F32)
        goes_to.append(jnp.sum(jnp.where(diagonal, line, 0.0), axis=1, keepdims=True))
    for b in range(parts):
        wide = (blocks, one_hots.shape[2])
        source = lax.broadcasted_iota(jnp.int32, wide, 0)
        lane = lax.broadcasted_iota(jnp.int32, wide, 1)
        line = jnp.zeros((1, wide[1]), F32)
        for h in range(2):
            for k in range(slots):
                low = (h * slots + k) * col_count
                here = (source - b * col_count == lane - low) & (lane >= low)
                here = here & (lane < low + col_count)
                line = line + jnp.sum(jnp.where(here, goes_to[k], 0.0), axis=0, keepdims=True)
        target = lax.broadcasted_iota(jnp.int32, one_hots.shape[1:], 0).astype(F32) + 1.0
        one_hots[b] = jnp.where(target == line, 1.0, 0.0).astype(BF16)

    w_copy.wait()
    tile = min(256, fout)

    def node_part(b, c):
        got = rg.at[b, pl.ds(0, fin - fin_dev)]
        pltpu.make_async_copy(got, got, fwd_recv.at[b]).wait()
        rows = rg[b]
        label = lab_ref[pl.ds(b * col_count + col, 1), :]
        one_hot = jnp.where(
            lax.broadcasted_iota(jnp.int32, (classes, blk), 0) == label, 1.0, 0.0
        ).astype(BF16)
        for j in range(fout // tile):
            at = pl.ds(j * tile, tile)
            hidden = lax.dot_general(
                rows, w[:, at], (((0,), (0,)), ((), ())), preferred_element_type=F32
            )
            target = lax.dot_general(
                one_hot, le_ref[:, at], (((0,), (0,)), ((), ())), preferred_element_type=F32
            )
            sigma = 1.0 / (1.0 + jnp.exp(-hidden))
            slope = sigma * (1.0 + hidden * (1.0 - sigma))
            gh[b, :, at] = (slope * target).astype(BF16)
        grad = gh[b]
        step = min(256, fin)
        for m in range(fin // step):
            part = lax.dot_general(
                w[pl.ds(m * step, step), :],
                grad,
                (((1,), (1,)), ((), ())),
                preferred_element_type=F32,
            ).astype(BF16)
            per = step // fin_dev
            ga[b, pl.ds(m * per, per)] = part.reshape(per, fin_dev, blk)

        def send(s, c):
            d = col_peer(s)
            pltpu.make_async_remote_copy(
                ga.at[b, d],
                ret.at[b, col],
                bwd_send,
                bwd_recv.at[b],
                device_id={"col": d},
                device_id_type=MESH,
            ).start()
            return c

        lax.fori_loop(1, col_count, send, 0)
        ret[b, col] = ga[b, col]
        return c

    lax.fori_loop(0, parts, node_part, 0)

    entries = slots * col_count
    f_rows = total_f.shape[0] // fin_dev

    def spread(b):
        got = ret.at[b, pl.ds(0, col_count - 1)]
        pltpu.make_async_copy(got, got, bwd_recv.at[b]).wait()
        several = 4

        def make(g, c):
            for t in range(several):
                d = g * several + t
                term = lax.dot_general(
                    ret[b, d], adj[b, d], (((1,), (1,)), ((), ())), preferred_element_type=F32
                )
                for k in range(slots):
                    at = pl.multiple_of((k * col_count + d) * fin_dev, fin_dev)
                    terms[pl.ds(at, fin_dev), :] = term[:, k * blk : (k + 1) * blk]
            return c

        lax.fori_loop(0, col_count // several, make, 0)
        table = one_hots[b]

        def add(p, c):
            for t in range(2):
                f = (p * 2 + t) * 2
                term = jnp.concatenate(
                    [terms[pl.ds(f + h, entries, stride=fin_dev), :] for h in range(2)], axis=1
                )
                high = term.astype(BF16)
                low = (term - high.astype(F32)).astype(BF16)
                part = jnp.dot(
                    table, jnp.concatenate([high, low], axis=0), preferred_element_type=F32
                )
                for h in range(2):
                    at = pl.ds(pl.multiple_of((f + h) * f_rows, 8), f_rows)
                    piece = part[:, h * blk : (h + 1) * blk]
                    total_f[at, :] = piece if b == 0 else total_f[at, :] + piece
            return c

        lax.fori_loop(0, fin_dev // 4, add, 0)

    chunks, zc = core_out.shape[0], core_out.shape[1]
    pair = 16 // rows_x
    rows_c = zc * 2 * fin_dev

    def weight_part(g):
        at = pl.ds(g * rows_c, rows_c)
        left = jnp.concatenate([rg[b, at, :] for b in range(parts)], axis=1)

        def columns(j, c):
            at = pl.ds(pl.multiple_of(j * tile, tile), tile)
            right = jnp.concatenate([gh[b, :, at] for b in range(parts)], axis=0)
            part = jnp.dot(left, right, preferred_element_type=F32)
            wp[g, :, :, :, at] = part.reshape(zc, 2, fin_dev, tile)
            return c

        lax.fori_loop(0, fout // tile, columns, 0)

        def round_core(i, c):
            core_out[g, i] = wp[g, i, 1 - core].astype(BF16)
            return c

        lax.fori_loop(0, zc, round_core, 0)

    def to_core(g):
        return pltpu.make_async_remote_copy(
            core_out.at[g],
            core_in.at[g],
            red_send.at[0, g],
            red_recv.at[0, g],
            device_id={"col": z * 2 + 1 - core},
            device_id_type=MESH,
        )

    def send_x(g):
        to_core(g).wait_recv()

        def round_x(i, c):
            sums = []
            for t in range(pair):
                total = wp[g, i * pair + t, core] + core_in[g, i * pair + t].astype(F32)
                wp[g, i * pair + t, core] = total
                sums.append(total)
            for k in range(NX):
                piece = jnp.concatenate([v[k * rows_x : (k + 1) * rows_x] for v in sums], axis=0)
                x_out[g, k, pl.ds(pl.multiple_of(i * 16, 16), 16), :] = piece.astype(BF16)
            return c

        lax.fori_loop(0, zc // pair, round_x, 0)
        for s in range(1, NX):
            pltpu.make_async_remote_copy(
                x_out.at[g, lax.rem(x + s, NX)],
                x_in.at[g, s - 1],
                red_send.at[1, g],
                red_recv.at[1, g],
                device_id={"row": x_peer(s)},
                device_id_type=MESH,
            ).start()

    def send_y(g):
        pltpu.make_async_copy(x_in.at[g], x_in.at[g], red_recv.at[1, g]).wait()

        def round_y(i, c):
            at = pl.ds(pl.multiple_of(i * 16, 16), 16)
            own = pl.ds(pl.multiple_of(x * rows_x, rows_x), rows_x)
            total = jnp.concatenate(
                [wp[g, i * pair + t, core, own, :] for t in range(pair)], axis=0
            )
            for s in range(NX - 1):
                total = total + x_in[g, s, at, :].astype(F32)
            for k in range(ny):
                piece = total[:, k * cols_y : (k + 1) * cols_y]
                q_own[g, k, at, :] = piece
                y_out[g, k, at, :] = piece.astype(BF16)
            return c

        lax.fori_loop(0, zc // pair, round_y, 0)

        def one(s, c):
            pltpu.make_async_remote_copy(
                y_out.at[g, lax.rem(y + s, ny)],
                y_in.at[g, s - 1],
                red_send.at[2, g],
                red_recv.at[2, g],
                device_id={"row": y_peer(s)},
                device_id_type=MESH,
            ).start()
            return c

        lax.fori_loop(1, ny, one, 0)

    for g in range(chunks):
        weight_part(g)
        to_core(g).start()
        if g > 0:
            send_x(g - 1)
    send_x(chunks - 1)
    spread(0)
    for g in range(chunks):
        send_y(g)
    for b in range(1, parts - 1):
        spread(b)

    for g in range(chunks):
        pltpu.make_async_copy(y_in.at[g], y_in.at[g], red_recv.at[2, g]).wait()
        total = q_own[g, y]
        for s in range(ny - 1):
            total = total + y_in[g, s].astype(F32)
        z_out[g * zc : (g + 1) * zc] = total.reshape(zc, rows_x, cols_y)

    def send_z(s, c):
        other = lax.rem(z + s, nz)
        pltpu.make_async_remote_copy(
            z_out.at[other],
            z_in.at[s - 1],
            last_send.at[0],
            last_recv.at[0],
            device_id={"col": other * 2 + core},
            device_id_type=MESH,
        ).start()
        return c

    lax.fori_loop(1, nz, send_z, 0)
    spread(parts - 1)
    pltpu.make_async_copy(z_in, z_in, last_recv.at[0]).wait()
    total = z_out[z]
    for s in range(nz - 1):
        total = total + z_in[s]
    shared[row] = total * factor

    def share(s, c):
        pltpu.make_async_remote_copy(
            shared.at[row],
            shared.at[row],
            last_send.at[1],
            last_recv.at[1],
            device_id={"row": row_peer(s)},
            device_id_type=MESH,
        ).start()
        return c

    lax.fori_loop(1, row_count, share, 0)
    for k in range(blocks):
        grad = total_f[pl.ds(k, fin_dev, stride=f_rows), :]
        fg_ref[:, k * blk : (k + 1) * blk] = grad.astype(BF16)
    got = shared.at[pl.ds(0, row_count - 1)]
    pltpu.make_async_copy(got, got, last_recv.at[1]).wait()
    for k in range(NX):
        wg_ref[k * rows_x : (k + 1) * rows_x, :] = jnp.concatenate(
            [shared[t * NX + k] for t in range(ny)], axis=1
        )

    sent = agg.at[:, pl.ds(0, col_count - 1)]
    pltpu.make_async_copy(sent, sent, fwd_send).wait()
    sent = ga.at[:, pl.ds(0, col_count - 1)]
    pltpu.make_async_copy(sent, sent, bwd_send).wait()
    for g in range(chunks):
        to_core(g).wait_send()
        pltpu.make_async_copy(x_in.at[g], x_in.at[g], red_send.at[1, g]).wait()
        pltpu.make_async_copy(y_in.at[g], y_in.at[g], red_send.at[2, g]).wait()
    pltpu.make_async_copy(z_in, z_in, last_send.at[0]).wait()
    sent = shared.at[pl.ds(0, row_count - 1)]
    pltpu.make_async_copy(sent, sent, last_send.at[1]).wait()


def write_kernel(wg_ref, fg_ref, wg_out, fg_out, sems):
    first = pltpu.make_async_copy(wg_ref, wg_out, sems.at[0])
    second = pltpu.make_async_copy(fg_ref, fg_out, sems.at[1])
    first.start()
    second.start()
    first.wait()
    second.wait()


def shards(features, adj_values, neighbours, counts, labels, layer_weight, label_embed):
    fin_dev, slab_nodes = features.shape
    blocks, slots, blk, _ = adj_values.shape
    fin, fout = layer_weight.shape
    col_count, row_count = lax.axis_size("col"), lax.axis_size("row")
    ny, nz = row_count // NX, col_count // 2
    rows_x, cols_y = fin_dev // NX, fout // ny
    parts = blocks // col_count
    factor = 1.0 / math.sqrt(slab_nodes * row_count)
    in_vmem = pl.BlockSpec(memory_space=pltpu.VMEM)
    in_smem = pl.BlockSpec(memory_space=pltpu.SMEM)
    anywhere = pl.BlockSpec(memory_space=pl.ANY)
    pieces = 4
    zc = 4 if nz % 4 == 0 and nz > 4 else 2
    chunks = nz // zc
    rows_c = zc * rows_x
    f_rows = -(-blocks // 16) * 16
    dma = pltpu.SemaphoreType.DMA

    weight_grad, feature_grad = pl.pallas_call(
        functools.partial(exchange_kernel, col_count, row_count, factor),
        out_shape=(
            jax.ShapeDtypeStruct((fin_dev, fout), F32),
            jax.ShapeDtypeStruct((fin_dev, slab_nodes), BF16),
        ),
        in_specs=[in_smem] * 2 + [in_vmem] * 5 + [anywhere] * 2,
        out_specs=(in_vmem, in_vmem),
        scratch_shapes=[
            pltpu.VMEM((blocks, fin_dev, blk), BF16),
            pltpu.VMEM((parts, col_count, slots * blk, blk), BF16),
            pltpu.VMEM((fin, fout), BF16),
            pltpu.VMEM((parts, col_count, fin_dev, blk), BF16),
            pltpu.VMEM((parts, fin, blk), BF16),
            pltpu.VMEM((parts, blk, fout), BF16),
            pltpu.VMEM((parts, col_count, fin_dev, blk), BF16),
            pltpu.VMEM((parts, col_count, fin_dev, blk), BF16),
            pltpu.VMEM((parts, f_rows, 2 * slots * col_count), BF16),
            pltpu.VMEM((slots * col_count * fin_dev, blk), F32),
            pltpu.VMEM((fin_dev * f_rows, blk), F32),
            pltpu.VMEM((chunks, zc, 2, fin_dev, fout), F32),
            pltpu.VMEM((chunks, zc, fin_dev, fout), BF16),
            pltpu.VMEM((chunks, zc, fin_dev, fout), BF16),
            pltpu.VMEM((chunks, NX, rows_c, fout), BF16),
            pltpu.VMEM((chunks, NX - 1, rows_c, fout), BF16),
            pltpu.VMEM((chunks, ny, rows_c, cols_y), F32),
            pltpu.VMEM((chunks, ny, rows_c, cols_y), BF16),
            pltpu.VMEM((chunks, ny - 1, rows_c, cols_y), BF16),
            pltpu.VMEM((nz, rows_x, cols_y), F32),
            pltpu.VMEM((nz - 1, rows_x, cols_y), F32),
            pltpu.VMEM((row_count, rows_x, cols_y), F32),
            dma((parts, pieces)),
            dma,
            dma,
            dma((parts,)),
            dma,
            dma((parts,)),
            dma((3, chunks)),
            dma((3, chunks)),
            dma((2,)),
            dma((2,)),
        ],
        compiler_params=pltpu.CompilerParams(
            collective_id=0, has_side_effects=True, vmem_limit_bytes=VMEM_LIMIT
        ),
        name="exchange",
    )(
        neighbours.T,
        counts,
        neighbours.T,
        counts.reshape(1, blocks),
        features,
        labels.reshape(blocks, blk),
        label_embed,
        adj_values.reshape(parts, col_count, slots * blk, blk),
        layer_weight,
    )
    return pl.pallas_call(
        write_kernel,
        out_shape=(
            jax.ShapeDtypeStruct((fin_dev, fout), F32),
            jax.ShapeDtypeStruct((fin_dev, slab_nodes), BF16),
        ),
        in_specs=[anywhere] * 2,
        out_specs=(anywhere, anywhere),
        scratch_shapes=[dma((2,))],
        compiler_params=pltpu.CompilerParams(vmem_limit_bytes=63 * 1024 * 1024),
        name="write",
    )(weight_grad, feature_grad)


def solution(mesh):
    return jax.shard_map(
        shards,
        mesh=mesh,
        in_specs=(
            P("col", "row"),
            P("row", None, None, None),
            P("row", None),
            P("row"),
            P("row"),
            P(),
            P(),
        ),
        out_specs=(P("col", None), P("col", "row")),
        check_vma=False,
    )
```

```python
import functools
import math

import jax
import jax.numpy as jnp
from jax import lax
from jax.experimental import pallas as pl
from jax.experimental.pallas import tpu as pltpu
from jax.sharding import PartitionSpec as P

NX = 4
BF16, F32 = jnp.bfloat16, jnp.float32
MESH = pl.DeviceIdType.MESH
VMEM_LIMIT = 56 * 1024 * 1024


def exchange_kernel(
    col_count,
    row_count,
    factor,
    nbr_ref,
    cnt_ref,
    nbr_rows,
    cnt_row,
    x_ref,
    lab_ref,
    le_ref,
    adj_hbm,
    w_hbm,
    wg_ref,
    fg_ref,
    x_blocks,
    adj,
    w,
    agg,
    rg,
    gh,
    ga,
    ret,
    one_hots,
    terms,
    total_f,
    wp,
    core_out,
    core_in,
    x_out,
    x_in,
    q_own,
    y_out,
    y_in,
    first_y_out,
    first_y_in,
    first_own,
    first_x_out,
    first_x_in,
    z_out,
    z_in,
    shared,
    adj_sem,
    w_sem,
    fwd_send,
    fwd_recv,
    bwd_send,
    bwd_recv,
    red_send,
    red_recv,
    last_send,
    last_recv,
):
    parts = agg.shape[0]
    fin_dev = x_ref.shape[0]
    fin, fout = w.shape
    slots = nbr_ref.shape[0]
    blocks = nbr_ref.shape[1]
    blk = x_ref.shape[1] // blocks
    ny, nz = row_count // NX, col_count // 2
    rows_x, cols_y = fin_dev // NX, fout // ny
    classes = le_ref.shape[0]

    col, row = lax.axis_index("col"), lax.axis_index("row")
    z, core = col // 2, lax.rem(col, 2)
    y, x = row // NX, lax.rem(row, NX)

    def col_peer(s):
        return lax.rem(col + s, col_count)

    def x_peer(s):
        return y * NX + lax.rem(x + s, NX)

    def row_peer(s):
        return lax.rem(row + s, row_count)

    def y_peer(s):
        return lax.rem(y + s, ny) * NX + x

    barrier = pltpu.get_barrier_semaphore()

    def greet_col(s, c):
        pl.semaphore_signal(barrier, inc=1, device_id={"col": col_peer(s)}, device_id_type=MESH)
        return c

    lax.fori_loop(1, col_count, greet_col, 0)
    def greet_row(s, c):
        pl.semaphore_signal(barrier, inc=1, device_id={"row": row_peer(s)}, device_id_type=MESH)
        return c

    lax.fori_loop(1, row_count, greet_row, 0)

    pieces = adj_sem.shape[1]
    width = col_count // pieces

    def adj_copy(b, g):
        at = pl.ds(g * width, width)
        return pltpu.make_async_copy(adj_hbm.at[b, at], adj.at[b, at], adj_sem.at[b, g])

    def group(g):
        return lax.rem(col // width + g, pieces)

    for b in range(parts):
        for g in range(pieces):
            adj_copy(b, group(g)).start()
    w_copy = pltpu.make_async_copy(w_hbm, w, w_sem)
    w_copy.start()

    for k in range(blocks):
        x_blocks[k] = x_ref[:, k * blk : (k + 1) * blk]

    def aggregate(b, g):
        adj_copy(b, g).wait()

        def one(d, c):
            i = b * col_count + d
            count = cnt_ref[i]
            picked = []
            for k in range(slots):
                live = jnp.clip(count - k, 0, 1).astype(F32)
                picked.append(x_blocks[nbr_ref[k, i]] * jnp.full((fin_dev, blk), live).astype(BF16))
            total = jnp.dot(
                jnp.concatenate(picked, axis=1), adj[b, d], preferred_element_type=F32
            )
            agg[b, d] = total.astype(BF16)
            return c

        for t in range(width):
            one(g * width + t, 0)

    def send_forward(b, g):
        def one(t, c):
            d = g * width + lax.rem(col + t, width)

            @pl.when(d != col)
            def _():
                pltpu.make_async_remote_copy(
                    agg.at[b, d],
                    rg.at[b, pl.ds(col * fin_dev, fin_dev)],
                    fwd_send,
                    fwd_recv.at[b],
                    device_id={"col": d},
                    device_id_type=MESH,
                ).start()

            return c

        lax.fori_loop(0, width, one, 0)

    aggregate(0, group(0))
    pl.semaphore_wait(barrier, (col_count - 1) + (row_count - 1))
    send_forward(0, group(0))
    for b in range(parts):

        def both(g, c, b=b):
            aggregate(b, group(g))
            send_forward(b, group(g))
            return c

        lax.fori_loop(1 if b == 0 else 0, pieces, both, 0)
        rg[b, pl.ds(pl.multiple_of(col * fin_dev, fin_dev), fin_dev), :] = agg[b, col]

    square = (blocks, blocks)
    diagonal = lax.broadcasted_iota(jnp.int32, square, 0) == lax.broadcasted_iota(jnp.int32, square, 1)
    goes_to = []
    for k in range(slots):
        line = jnp.where(cnt_row[...] > k, nbr_rows[k : k + 1, :] + 1, 0).astype(F32)
        goes_to.append(jnp.sum(jnp.where(diagonal, line, 0.0), axis=1, keepdims=True))
    for b in range(parts):
        wide = (blocks, one_hots.shape[2])
        source = lax.broadcasted_iota(jnp.int32, wide, 0)
        lane = lax.broadcasted_iota(jnp.int32, wide, 1)
        line = jnp.zeros((1, wide[1]), F32)
        for h in range(2):
            for k in range(slots):
                low = (h * slots + k) * col_count
                here = (source - b * col_count == lane - low) & (lane >= low)
                here = here & (lane < low + col_count)
                line = line + jnp.sum(jnp.where(here, goes_to[k], 0.0), axis=0, keepdims=True)
        target = lax.broadcasted_iota(jnp.int32, one_hots.shape[1:], 0).astype(F32) + 1.0
        one_hots[b] = jnp.where(target == line, 1.0, 0.0).astype(BF16)

    w_copy.wait()
    tile = min(256, fout)

    def grad_part(b, c):
        got = rg.at[b, pl.ds(0, fin - fin_dev)]
        pltpu.make_async_copy(got, got, fwd_recv.at[b]).wait()
        rows = rg[b]
        label = lab_ref[pl.ds(b * col_count + col, 1), :]
        one_hot = jnp.where(
            lax.broadcasted_iota(jnp.int32, (classes, blk), 0) == label, 1.0, 0.0
        ).astype(BF16)
        for j in range(fout // tile):
            at = pl.ds(j * tile, tile)
            hidden = lax.dot_general(
                rows, w[:, at], (((0,), (0,)), ((), ())), preferred_element_type=F32
            )
            target = lax.dot_general(
                one_hot, le_ref[:, at], (((0,), (0,)), ((), ())), preferred_element_type=F32
            )
            sigma = 1.0 / (1.0 + jnp.exp(-hidden))
            slope = sigma * (1.0 + hidden * (1.0 - sigma))
            gh[b, :, at] = (slope * target).astype(BF16)
        return c

    def back_part(b, c):
        grad = gh[b]
        step = min(256, fin)
        for m in range(fin // step):
            part = lax.dot_general(
                w[pl.ds(m * step, step), :],
                grad,
                (((1,), (1,)), ((), ())),
                preferred_element_type=F32,
            ).astype(BF16)
            per = step // fin_dev
            ga[b, pl.ds(m * per, per)] = part.reshape(per, fin_dev, blk)
        ret[b, col] = ga[b, col]
        return c

    def send_back(b):
        def send(s, c):
            d = col_peer(s)
            pltpu.make_async_remote_copy(
                ga.at[b, d],
                ret.at[b, col],
                bwd_send,
                bwd_recv.at[b],
                device_id={"col": d},
                device_id_type=MESH,
            ).start()
            return c

        lax.fori_loop(1, col_count, send, 0)

    def early(b, c):
        grad_part(b, c)
        back_part(b, c)
        send_back(b)
        return c

    last = parts - 1
    lax.fori_loop(0, last, early, 0)
    grad_part(last, 0)

    entries = slots * col_count
    f_rows = total_f.shape[0] // fin_dev

    def spread(b):
        got = ret.at[b, pl.ds(0, col_count - 1)]
        pltpu.make_async_copy(got, got, bwd_recv.at[b]).wait()
        several = 4

        def make(g, c):
            for t in range(several):
                d = g * several + t
                term = lax.dot_general(
                    ret[b, d], adj[b, d], (((1,), (1,)), ((), ())), preferred_element_type=F32
                )
                for k in range(slots):
                    at = pl.multiple_of((k * col_count + d) * fin_dev, fin_dev)
                    terms[pl.ds(at, fin_dev), :] = term[:, k * blk : (k + 1) * blk]
            return c

        lax.fori_loop(0, col_count // several, make, 0)
        table = one_hots[b]

        def add(p, c):
            for t in range(2):
                f = (p * 2 + t) * 2
                term = jnp.concatenate(
                    [terms[pl.ds(f + h, entries, stride=fin_dev), :] for h in range(2)], axis=1
                )
                high = term.astype(BF16)
                low = (term - high.astype(F32)).astype(BF16)
                part = jnp.dot(
                    table, jnp.concatenate([high, low], axis=0), preferred_element_type=F32
                )
                for h in range(2):
                    at = pl.ds(pl.multiple_of((f + h) * f_rows, 8), f_rows)
                    piece = part[:, h * blk : (h + 1) * blk]
                    total_f[at, :] = piece if b == 0 else total_f[at, :] + piece
            return c

        lax.fori_loop(0, fin_dev // 4, add, 0)

    chunks, zc = core_out.shape[0], core_out.shape[1]
    pair = 16 // rows_x
    rows_c = zc * 2 * fin_dev

    def weight_part(g):
        at = pl.ds(g * rows_c, rows_c)
        left = jnp.concatenate([rg[b, at, :] for b in range(parts)], axis=1)

        def columns(j, c):
            at = pl.ds(pl.multiple_of(j * tile, tile), tile)
            right = jnp.concatenate([gh[b, :, at] for b in range(parts)], axis=0)
            part = jnp.dot(left, right, preferred_element_type=F32)
            wp[g, :, :, :, at] = part.reshape(zc, 2, fin_dev, tile)
            return c

        lax.fori_loop(0, fout // tile, columns, 0)

        def round_core(i, c):
            core_out[g, i] = wp[g, i, 1 - core].astype(BF16)
            return c

        lax.fori_loop(0, zc, round_core, 0)

    def to_core(g):
        return pltpu.make_async_remote_copy(
            core_out.at[g],
            core_in.at[g],
            red_send.at[0, g],
            red_recv.at[0, g],
            device_id={"col": z * 2 + 1 - core},
            device_id_type=MESH,
        )

    def send_x(g):
        to_core(g).wait_recv()

        def round_x(i, c):
            sums = []
            for t in range(pair):
                total = wp[g, i * pair + t, core] + core_in[g, i * pair + t].astype(F32)
                wp[g, i * pair + t, core] = total
                sums.append(total)
            for k in range(NX):
                piece = jnp.concatenate([v[k * rows_x : (k + 1) * rows_x] for v in sums], axis=0)
                x_out[g, k, pl.ds(pl.multiple_of(i * 16, 16), 16), :] = piece.astype(BF16)
            return c

        lax.fori_loop(0, zc // pair, round_x, 0)
        for s in range(1, NX):
            pltpu.make_async_remote_copy(
                x_out.at[g, lax.rem(x + s, NX)],
                x_in.at[g, s - 1],
                red_send.at[1, g],
                red_recv.at[1, g],
                device_id={"row": x_peer(s)},
                device_id_type=MESH,
            ).start()

    def send_y(g):
        pltpu.make_async_copy(x_in.at[g], x_in.at[g], red_recv.at[1, g]).wait()

        def round_y(i, c):
            at = pl.ds(pl.multiple_of(i * 16, 16), 16)
            own = pl.ds(pl.multiple_of(x * rows_x, rows_x), rows_x)
            total = jnp.concatenate(
                [wp[g, i * pair + t, core, own, :] for t in range(pair)], axis=0
            )
            for s in range(NX - 1):
                total = total + x_in[g, s, at, :].astype(F32)
            for k in range(ny):
                piece = total[:, k * cols_y : (k + 1) * cols_y]
                q_own[g, k, at, :] = piece
                y_out[g, k, at, :] = piece.astype(BF16)
            return c

        lax.fori_loop(0, zc // pair, round_y, 0)

        def one(s, c):
            pltpu.make_async_remote_copy(
                y_out.at[g, lax.rem(y + s, ny)],
                y_in.at[g, s - 1],
                red_send.at[2, g],
                red_recv.at[2, g],
                device_id={"row": y_peer(s)},
                device_id_type=MESH,
            ).start()
            return c

        lax.fori_loop(1, ny, one, 0)

    def send_y_first():
        to_core(0).wait_recv()

        def one_row(i, c):
            total = wp[0, i, core] + core_in[0, i].astype(F32)
            wp[0, i, core] = total
            at = pl.ds(pl.multiple_of(i * fin_dev, fin_dev), fin_dev)
            for k in range(ny):
                first_y_out[k, at, :] = total[:, k * cols_y : (k + 1) * cols_y].astype(BF16)
            return c

        lax.fori_loop(0, zc, one_row, 0)

        def one(s, c):
            pltpu.make_async_remote_copy(
                first_y_out.at[lax.rem(y + s, ny)],
                first_y_in.at[s - 1],
                red_send.at[2, 0],
                red_recv.at[2, 0],
                device_id={"row": y_peer(s)},
                device_id_type=MESH,
            ).start()
            return c

        lax.fori_loop(1, ny, one, 0)

    def send_x_second():
        pltpu.make_async_copy(first_y_in, first_y_in, red_recv.at[2, 0]).wait()

        def some_rows(i, c):
            sums = []
            for t in range(pair):
                k = i * pair + t
                total = wp[0, k, core, :, pl.ds(pl.multiple_of(y * cols_y, cols_y), cols_y)]
                at = pl.ds(pl.multiple_of(k * fin_dev, fin_dev), fin_dev)
                for s in range(ny - 1):
                    total = total + first_y_in[s, at, :].astype(F32)
                sums.append(total)
            at = pl.ds(pl.multiple_of(i * 16, 16), 16)
            for k in range(NX):
                piece = jnp.concatenate([v[k * rows_x : (k + 1) * rows_x] for v in sums], axis=0)
                first_own[k, at, :] = piece
                first_x_out[k, at, :] = piece.astype(BF16)
            return c

        lax.fori_loop(0, zc // pair, some_rows, 0)
        for s in range(1, NX):
            pltpu.make_async_remote_copy(
                first_x_out.at[lax.rem(x + s, NX)],
                first_x_in.at[s - 1],
                red_send.at[1, 0],
                red_recv.at[1, 0],
                device_id={"row": x_peer(s)},
                device_id_type=MESH,
            ).start()

    for g in range(chunks):
        weight_part(g)
        to_core(g).start()
        if g == 1:
            send_y_first()
        if g > 1:
            send_x(g - 1)
    send_x(chunks - 1)
    back_part(last, 0)
    send_back(last)
    spread(0)
    send_x_second()
    for g in range(1, chunks):
        send_y(g)

    pltpu.make_async_copy(first_x_in, first_x_in, red_recv.at[1, 0]).wait()
    total = first_own[x]
    for s in range(NX - 1):
        total = total + first_x_in[s].astype(F32)
    z_out[0:zc] = total.reshape(zc, rows_x, cols_y)
    for g in range(1, chunks):
        pltpu.make_async_copy(y_in.at[g], y_in.at[g], red_recv.at[2, g]).wait()
        total = q_own[g, y]
        for s in range(ny - 1):
            total = total + y_in[g, s].astype(F32)
        z_out[g * zc : (g + 1) * zc] = total.reshape(zc, rows_x, cols_y)

    def send_z(s, c):
        other = lax.rem(z + s, nz)
        pltpu.make_async_remote_copy(
            z_out.at[other],
            z_in.at[s - 1],
            last_send.at[0],
            last_recv.at[0],
            device_id={"col": other * 2 + core},
            device_id_type=MESH,
        ).start()
        return c

    lax.fori_loop(1, nz, send_z, 0)
    for b in range(1, last):
        spread(b)
    pltpu.make_async_copy(z_in, z_in, last_recv.at[0]).wait()
    total = z_out[z]
    for s in range(nz - 1):
        total = total + z_in[s]
    shared[row] = total * factor

    def share(s, c):
        pltpu.make_async_remote_copy(
            shared.at[row],
            shared.at[row],
            last_send.at[1],
            last_recv.at[1],
            device_id={"row": row_peer(s)},
            device_id_type=MESH,
        ).start()
        return c

    lax.fori_loop(1, row_count, share, 0)
    spread(last)
    for k in range(blocks):
        grad = total_f[pl.ds(k, fin_dev, stride=f_rows), :]
        fg_ref[:, k * blk : (k + 1) * blk] = grad.astype(BF16)
    got = shared.at[pl.ds(0, row_count - 1)]
    pltpu.make_async_copy(got, got, last_recv.at[1]).wait()
    for k in range(NX):
        wg_ref[k * rows_x : (k + 1) * rows_x, :] = jnp.concatenate(
            [shared[t * NX + k] for t in range(ny)], axis=1
        )

    sent = agg.at[:, pl.ds(0, col_count - 1)]
    pltpu.make_async_copy(sent, sent, fwd_send).wait()
    sent = ga.at[:, pl.ds(0, col_count - 1)]
    pltpu.make_async_copy(sent, sent, bwd_send).wait()
    for g in range(chunks):
        to_core(g).wait_send()
        left_x = first_x_in if g == 0 else x_in.at[g]
        left_y = first_y_in if g == 0 else y_in.at[g]
        pltpu.make_async_copy(left_x, left_x, red_send.at[1, g]).wait()
        pltpu.make_async_copy(left_y, left_y, red_send.at[2, g]).wait()
    pltpu.make_async_copy(z_in, z_in, last_send.at[0]).wait()
    sent = shared.at[pl.ds(0, row_count - 1)]
    pltpu.make_async_copy(sent, sent, last_send.at[1]).wait()


def write_kernel(wg_ref, fg_ref, wg_out, fg_out):
    wg_out[...] = wg_ref[...]
    fg_out[...] = fg_ref[...]


def shards(features, adj_values, neighbours, counts, labels, layer_weight, label_embed):
    fin_dev, slab_nodes = features.shape
    blocks, slots, blk, _ = adj_values.shape
    fin, fout = layer_weight.shape
    col_count, row_count = lax.axis_size("col"), lax.axis_size("row")
    ny, nz = row_count // NX, col_count // 2
    rows_x, cols_y = fin_dev // NX, fout // ny
    parts = blocks // col_count
    factor = 1.0 / math.sqrt(slab_nodes * row_count)
    in_vmem = pl.BlockSpec(memory_space=pltpu.VMEM)
    in_smem = pl.BlockSpec(memory_space=pltpu.SMEM)
    anywhere = pl.BlockSpec(memory_space=pl.ANY)
    pieces = 4
    zc = 4 if nz % 4 == 0 and nz > 4 else 2
    chunks = nz // zc
    rows_c = zc * rows_x
    f_rows = -(-blocks // 16) * 16
    dma = pltpu.SemaphoreType.DMA

    weight_grad, feature_grad = pl.pallas_call(
        functools.partial(exchange_kernel, col_count, row_count, factor),
        out_shape=(
            jax.ShapeDtypeStruct((fin_dev, fout), F32),
            jax.ShapeDtypeStruct((fin_dev, slab_nodes), BF16),
        ),
        in_specs=[in_smem] * 2 + [in_vmem] * 5 + [anywhere] * 2,
        out_specs=(in_vmem, in_vmem),
        scratch_shapes=[
            pltpu.VMEM((blocks, fin_dev, blk), BF16),
            pltpu.VMEM((parts, col_count, slots * blk, blk), BF16),
            pltpu.VMEM((fin, fout), BF16),
            pltpu.VMEM((parts, col_count, fin_dev, blk), BF16),
            pltpu.VMEM((parts, fin, blk), BF16),
            pltpu.VMEM((parts, blk, fout), BF16),
            pltpu.VMEM((parts, col_count, fin_dev, blk), BF16),
            pltpu.VMEM((parts, col_count, fin_dev, blk), BF16),
            pltpu.VMEM((parts, f_rows, 2 * slots * col_count), BF16),
            pltpu.VMEM((slots * col_count * fin_dev, blk), F32),
            pltpu.VMEM((fin_dev * f_rows, blk), F32),
            pltpu.VMEM((chunks, zc, 2, fin_dev, fout), F32),
            pltpu.VMEM((chunks, zc, fin_dev, fout), BF16),
            pltpu.VMEM((chunks, zc, fin_dev, fout), BF16),
            pltpu.VMEM((chunks, NX, rows_c, fout), BF16),
            pltpu.VMEM((chunks, NX - 1, rows_c, fout), BF16),
            pltpu.VMEM((chunks, ny, rows_c, cols_y), F32),
            pltpu.VMEM((chunks, ny, rows_c, cols_y), BF16),
            pltpu.VMEM((chunks, ny - 1, rows_c, cols_y), BF16),
            pltpu.VMEM((ny, zc * fin_dev, cols_y), BF16),
            pltpu.VMEM((ny - 1, zc * fin_dev, cols_y), BF16),
            pltpu.VMEM((NX, rows_c, cols_y), F32),
            pltpu.VMEM((NX, rows_c, cols_y), BF16),
            pltpu.VMEM((NX - 1, rows_c, cols_y), BF16),
            pltpu.VMEM((nz, rows_x, cols_y), F32),
            pltpu.VMEM((nz - 1, rows_x, cols_y), F32),
            pltpu.VMEM((row_count, rows_x, cols_y), F32),
            dma((parts, pieces)),
            dma,
            dma,
            dma((parts,)),
            dma,
            dma((parts,)),
            dma((3, chunks)),
            dma((3, chunks)),
            dma((2,)),
            dma((2,)),
        ],
        compiler_params=pltpu.CompilerParams(
            collective_id=0, has_side_effects=True, vmem_limit_bytes=VMEM_LIMIT
        ),
        name="exchange",
    )(
        neighbours.T,
        counts,
        neighbours.T,
        counts.reshape(1, blocks),
        features,
        labels.reshape(blocks, blk),
        label_embed,
        adj_values.reshape(parts, col_count, slots * blk, blk),
        layer_weight,
    )
    return pl.pallas_call(
        write_kernel,
        out_shape=(
            jax.ShapeDtypeStruct((fin_dev, fout), F32),
            jax.ShapeDtypeStruct((fin_dev, slab_nodes), BF16),
        ),
        in_specs=[in_vmem] * 2,
        out_specs=(in_vmem, in_vmem),
        name="write",
    )(weight_grad, feature_grad)


def solution(mesh):
    return jax.shard_map(
        shards,
        mesh=mesh,
        in_specs=(
            P("col", "row"),
            P("row", None, None, None),
            P("row", None),
            P("row"),
            P("row"),
            P(),
            P(),
        ),
        out_specs=(P("col", None), P("col", "row")),
        check_vma=False,
    )
```

```python
import functools
import math

import jax
import jax.numpy as jnp
from jax import lax
from jax.experimental import pallas as pl
from jax.experimental.pallas import tpu as pltpu
from jax.sharding import PartitionSpec as P

NX = 4
BF16, F32 = jnp.bfloat16, jnp.float32
MESH = pl.DeviceIdType.MESH
VMEM_LIMIT = 56 * 1024 * 1024


def exchange_kernel(
    col_count,
    row_count,
    factor,
    nbr_ref,
    cnt_ref,
    nbr_rows,
    cnt_row,
    x_ref,
    lab_ref,
    le_ref,
    adj_hbm,
    w_hbm,
    wg_ref,
    fg_ref,
    x_blocks,
    adj,
    w,
    agg,
    rg,
    gh,
    ga,
    ret,
    one_hots,
    terms,
    total_f,
    wp,
    core_out,
    core_in,
    x_out,
    x_in,
    q_own,
    y_out,
    y_in,
    first_y_out,
    first_y_in,
    first_own,
    first_x_out,
    first_x_in,
    z_out,
    z_in,
    shared,
    adj_sem,
    w_sem,
    fwd_send,
    fwd_recv,
    bwd_send,
    bwd_recv,
    red_send,
    red_recv,
    last_send,
    last_recv,
):
    parts = agg.shape[0]
    fin_dev = x_ref.shape[0]
    fin, fout = w.shape
    slots = nbr_ref.shape[0]
    blocks = nbr_ref.shape[1]
    blk = x_ref.shape[1] // blocks
    ny, nz = row_count // NX, col_count // 2
    rows_x, cols_y = fin_dev // NX, fout // ny
    classes = le_ref.shape[0]

    col, row = lax.axis_index("col"), lax.axis_index("row")
    z, core = col // 2, lax.rem(col, 2)
    y, x = row // NX, lax.rem(row, NX)

    def col_peer(s):
        return lax.rem(col + s, col_count)

    def x_peer(s):
        return y * NX + lax.rem(x + s, NX)

    def far_first(t, count):
        return 1 + lax.rem(t + count // 2 - count // 8 - 1, count - 1)

    def row_peer(s):
        return lax.rem(row + s, row_count)

    def y_peer(s):
        return lax.rem(y + s, ny) * NX + x

    pieces = adj_sem.shape[1]
    width = col_count // pieces

    def adj_copy(b, g):
        at = pl.ds(g * width, width)
        return pltpu.make_async_copy(adj_hbm.at[b, at], adj.at[b, at], adj_sem.at[b, g])

    def group(g):
        return lax.rem(col // width + g, pieces)

    for b in range(parts):
        for g in range(pieces):
            adj_copy(b, group(g)).start()
    w_copy = pltpu.make_async_copy(w_hbm, w, w_sem)
    w_copy.start()

    barrier = pltpu.get_barrier_semaphore()

    def greet_col(s, c):
        pl.semaphore_signal(barrier, inc=1, device_id={"col": col_peer(s)}, device_id_type=MESH)
        return c

    lax.fori_loop(1, col_count, greet_col, 0)
    def greet_row(s, c):
        pl.semaphore_signal(barrier, inc=1, device_id={"row": row_peer(s)}, device_id_type=MESH)
        return c

    lax.fori_loop(1, row_count, greet_row, 0)

    for k in range(blocks):
        x_blocks[k] = x_ref[:, k * blk : (k + 1) * blk]

    def aggregate(b, g):
        adj_copy(b, g).wait()

        def one(d, c):
            i = b * col_count + d
            count = cnt_ref[i]
            picked = []
            for k in range(slots):
                live = jnp.clip(count - k, 0, 1).astype(F32)
                picked.append(x_blocks[nbr_ref[k, i]] * jnp.full((fin_dev, blk), live).astype(BF16))
            total = jnp.dot(
                jnp.concatenate(picked, axis=1), adj[b, d], preferred_element_type=F32
            )
            agg[b, d] = total.astype(BF16)
            return c

        for t in range(width):
            one(g * width + t, 0)

    def send_forward(b, g):
        def one(t, c):
            d = g * width + lax.rem(col + t, width)

            @pl.when(d != col)
            def _():
                pltpu.make_async_remote_copy(
                    agg.at[b, d],
                    rg.at[b, pl.ds(col * fin_dev, fin_dev)],
                    fwd_send,
                    fwd_recv.at[b],
                    device_id={"col": d},
                    device_id_type=MESH,
                ).start()

            return c

        lax.fori_loop(0, width, one, 0)

    aggregate(0, group(0))
    pl.semaphore_wait(barrier, (col_count - 1) + (row_count - 1))
    send_forward(0, group(0))
    for b in range(parts):

        def both(g, c, b=b):
            aggregate(b, group(g))
            send_forward(b, group(g))
            return c

        lax.fori_loop(1 if b == 0 else 0, pieces, both, 0)
        rg[b, pl.ds(pl.multiple_of(col * fin_dev, fin_dev), fin_dev), :] = agg[b, col]

    square = (blocks, blocks)
    diagonal = lax.broadcasted_iota(jnp.int32, square, 0) == lax.broadcasted_iota(jnp.int32, square, 1)
    goes_to = []
    for k in range(slots):
        line = jnp.where(cnt_row[...] > k, nbr_rows[k : k + 1, :] + 1, 0).astype(F32)
        goes_to.append(jnp.sum(jnp.where(diagonal, line, 0.0), axis=1, keepdims=True))
    for b in range(parts):
        wide = (blocks, one_hots.shape[2])
        source = lax.broadcasted_iota(jnp.int32, wide, 0)
        lane = lax.broadcasted_iota(jnp.int32, wide, 1)
        line = jnp.zeros((1, wide[1]), F32)
        for h in range(2):
            for k in range(slots):
                low = (h * slots + k) * col_count
                here = (source - b * col_count == lane - low) & (lane >= low)
                here = here & (lane < low + col_count)
                line = line + jnp.sum(jnp.where(here, goes_to[k], 0.0), axis=0, keepdims=True)
        target = lax.broadcasted_iota(jnp.int32, one_hots.shape[1:], 0).astype(F32) + 1.0
        one_hots[b] = jnp.where(target == line, 1.0, 0.0).astype(BF16)

    w_copy.wait()
    tile = min(256, fout)

    def grad_part(b, c):
        got = rg.at[b, pl.ds(0, fin - fin_dev)]
        pltpu.make_async_copy(got, got, fwd_recv.at[b]).wait()
        rows = rg[b]
        label = lab_ref[pl.ds(b * col_count + col, 1), :]
        one_hot = jnp.where(
            lax.broadcasted_iota(jnp.int32, (classes, blk), 0) == label, 1.0, 0.0
        ).astype(BF16)
        for j in range(fout // tile):
            at = pl.ds(j * tile, tile)
            hidden = lax.dot_general(
                rows, w[:, at], (((0,), (0,)), ((), ())), preferred_element_type=F32
            )
            target = lax.dot_general(
                one_hot, le_ref[:, at], (((0,), (0,)), ((), ())), preferred_element_type=F32
            )
            sigma = 1.0 / (1.0 + jnp.exp(-hidden))
            slope = sigma * (1.0 + hidden * (1.0 - sigma))
            gh[b, :, at] = (slope * target).astype(BF16)
        return c

    def back_part(b, c):
        grad = gh[b]
        step = min(256, fin)
        for m in range(fin // step):
            part = lax.dot_general(
                w[pl.ds(m * step, step), :],
                grad,
                (((1,), (1,)), ((), ())),
                preferred_element_type=F32,
            ).astype(BF16)
            per = step // fin_dev
            ga[b, pl.ds(m * per, per)] = part.reshape(per, fin_dev, blk)
        ret[b, col] = ga[b, col]
        return c

    def send_back(b):
        def send(s, c):
            d = col_peer(s)
            pltpu.make_async_remote_copy(
                ga.at[b, d],
                ret.at[b, col],
                bwd_send,
                bwd_recv.at[b],
                device_id={"col": d},
                device_id_type=MESH,
            ).start()
            return c

        lax.fori_loop(1, col_count, send, 0)

    def early(b, c):
        grad_part(b, c)
        back_part(b, c)
        send_back(b)
        return c

    last = parts - 1
    lax.fori_loop(0, last, early, 0)
    grad_part(last, 0)

    entries = slots * col_count
    f_rows = total_f.shape[0] // fin_dev

    def spread(b):
        got = ret.at[b, pl.ds(0, col_count - 1)]
        pltpu.make_async_copy(got, got, bwd_recv.at[b]).wait()
        several = 4

        def make(g, c):
            for t in range(several):
                d = g * several + t
                term = lax.dot_general(
                    ret[b, d], adj[b, d], (((1,), (1,)), ((), ())), preferred_element_type=F32
                )
                for k in range(slots):
                    at = pl.multiple_of((k * col_count + d) * fin_dev, fin_dev)
                    terms[pl.ds(at, fin_dev), :] = term[:, k * blk : (k + 1) * blk]
            return c

        lax.fori_loop(0, col_count // several, make, 0)
        table = one_hots[b]

        def add(p, c):
            for t in range(2):
                f = (p * 2 + t) * 2
                term = jnp.concatenate(
                    [terms[pl.ds(f + h, entries, stride=fin_dev), :] for h in range(2)], axis=1
                )
                high = term.astype(BF16)
                low = (term - high.astype(F32)).astype(BF16)
                part = jnp.dot(
                    table, jnp.concatenate([high, low], axis=0), preferred_element_type=F32
                )
                for h in range(2):
                    at = pl.ds(pl.multiple_of((f + h) * f_rows, 8), f_rows)
                    piece = part[:, h * blk : (h + 1) * blk]
                    total_f[at, :] = piece if b == 0 else total_f[at, :] + piece
            return c

        lax.fori_loop(0, fin_dev // 4, add, 0)

    chunks, zc = core_out.shape[0], core_out.shape[1]
    pair = 16 // rows_x
    rows_c = zc * 2 * fin_dev

    def weight_part(g):
        at = pl.ds(g * rows_c, rows_c)
        left = jnp.concatenate([rg[b, at, :] for b in range(parts)], axis=1)

        def columns(j, c):
            at = pl.ds(pl.multiple_of(j * tile, tile), tile)
            right = jnp.concatenate([gh[b, :, at] for b in range(parts)], axis=0)
            part = jnp.dot(left, right, preferred_element_type=F32)
            wp[g, :, :, :, at] = part.reshape(zc, 2, fin_dev, tile)
            return c

        lax.fori_loop(0, fout // tile, columns, 0)

        def round_core(i, c):
            core_out[g, i] = wp[g, i, 1 - core].astype(BF16)
            return c

        lax.fori_loop(0, zc, round_core, 0)

    def to_core(g):
        return pltpu.make_async_remote_copy(
            core_out.at[g],
            core_in.at[g],
            red_send.at[0, g],
            red_recv.at[0, g],
            device_id={"col": z * 2 + 1 - core},
            device_id_type=MESH,
        )

    def send_x(g):
        to_core(g).wait_recv()

        def round_x(i, c):
            sums = []
            for t in range(pair):
                total = wp[g, i * pair + t, core] + core_in[g, i * pair + t].astype(F32)
                wp[g, i * pair + t, core] = total
                sums.append(total)
            for k in range(NX):
                piece = jnp.concatenate([v[k * rows_x : (k + 1) * rows_x] for v in sums], axis=0)
                x_out[g, k, pl.ds(pl.multiple_of(i * 16, 16), 16), :] = piece.astype(BF16)
            return c

        lax.fori_loop(0, zc // pair, round_x, 0)
        for s in range(1, NX):
            pltpu.make_async_remote_copy(
                x_out.at[g, lax.rem(x + s, NX)],
                x_in.at[g, s - 1],
                red_send.at[1, g],
                red_recv.at[1, g],
                device_id={"row": x_peer(s)},
                device_id_type=MESH,
            ).start()

    def send_y(g):
        pltpu.make_async_copy(x_in.at[g], x_in.at[g], red_recv.at[1, g]).wait()

        def round_y(i, c):
            at = pl.ds(pl.multiple_of(i * 16, 16), 16)
            own = pl.ds(pl.multiple_of(x * rows_x, rows_x), rows_x)
            total = jnp.concatenate(
                [wp[g, i * pair + t, core, own, :] for t in range(pair)], axis=0
            )
            for s in range(NX - 1):
                total = total + x_in[g, s, at, :].astype(F32)
            for k in range(ny):
                piece = total[:, k * cols_y : (k + 1) * cols_y]
                q_own[g, k, at, :] = piece
                y_out[g, k, at, :] = piece.astype(BF16)
            return c

        lax.fori_loop(0, zc // pair, round_y, 0)

        def one(s, c):
            s = far_first(s, ny)
            pltpu.make_async_remote_copy(
                y_out.at[g, lax.rem(y + s, ny)],
                y_in.at[g, s - 1],
                red_send.at[2, g],
                red_recv.at[2, g],
                device_id={"row": y_peer(s)},
                device_id_type=MESH,
            ).start()
            return c

        lax.fori_loop(1, ny, one, 0)

    def send_y_first():
        to_core(0).wait_recv()

        def one_row(i, c):
            total = wp[0, i, core] + core_in[0, i].astype(F32)
            wp[0, i, core] = total
            at = pl.ds(pl.multiple_of(i * fin_dev, fin_dev), fin_dev)
            for k in range(ny):
                first_y_out[k, at, :] = total[:, k * cols_y : (k + 1) * cols_y].astype(BF16)
            return c

        lax.fori_loop(0, zc, one_row, 0)

        def one(s, c):
            s = far_first(s, ny)
            pltpu.make_async_remote_copy(
                first_y_out.at[lax.rem(y + s, ny)],
                first_y_in.at[s - 1],
                red_send.at[2, 0],
                red_recv.at[2, 0],
                device_id={"row": y_peer(s)},
                device_id_type=MESH,
            ).start()
            return c

        lax.fori_loop(1, ny, one, 0)

    def send_x_second():
        pltpu.make_async_copy(first_y_in, first_y_in, red_recv.at[2, 0]).wait()

        def some_rows(i, c):
            sums = []
            for t in range(pair):
                k = i * pair + t
                total = wp[0, k, core, :, pl.ds(pl.multiple_of(y * cols_y, cols_y), cols_y)]
                at = pl.ds(pl.multiple_of(k * fin_dev, fin_dev), fin_dev)
                for s in range(ny - 1):
                    total = total + first_y_in[s, at, :].astype(F32)
                sums.append(total)
            at = pl.ds(pl.multiple_of(i * 16, 16), 16)
            for k in range(NX):
                piece = jnp.concatenate([v[k * rows_x : (k + 1) * rows_x] for v in sums], axis=0)
                first_own[k, at, :] = piece
                first_x_out[k, at, :] = piece.astype(BF16)
            return c

        lax.fori_loop(0, zc // pair, some_rows, 0)
        for s in range(1, NX):
            pltpu.make_async_remote_copy(
                first_x_out.at[lax.rem(x + s, NX)],
                first_x_in.at[s - 1],
                red_send.at[1, 0],
                red_recv.at[1, 0],
                device_id={"row": x_peer(s)},
                device_id_type=MESH,
            ).start()

    for g in range(chunks):
        weight_part(g)
        to_core(g).start()
        if g == 1:
            send_y_first()
        if g > 1:
            send_x(g - 1)
    send_x(chunks - 1)
    back_part(last, 0)
    send_back(last)
    spread(0)
    send_x_second()
    for g in range(1, chunks):
        send_y(g)

    pltpu.make_async_copy(first_x_in, first_x_in, red_recv.at[1, 0]).wait()
    total = first_own[x]
    for s in range(NX - 1):
        total = total + first_x_in[s].astype(F32)
    z_out[0:zc] = total.reshape(zc, rows_x, cols_y)
    for g in range(1, chunks):
        pltpu.make_async_copy(y_in.at[g], y_in.at[g], red_recv.at[2, g]).wait()
        total = q_own[g, y]
        for s in range(ny - 1):
            total = total + y_in[g, s].astype(F32)
        z_out[g * zc : (g + 1) * zc] = total.reshape(zc, rows_x, cols_y)

    def send_z(s, c):
        s = far_first(s, nz)
        other = lax.rem(z + s, nz)
        pltpu.make_async_remote_copy(
            z_out.at[other],
            z_in.at[s - 1],
            last_send.at[0],
            last_recv.at[0],
            device_id={"col": other * 2 + core},
            device_id_type=MESH,
        ).start()
        return c

    lax.fori_loop(1, nz, send_z, 0)
    for b in range(1, last):
        spread(b)
    pltpu.make_async_copy(z_in, z_in, last_recv.at[0]).wait()
    total = z_out[z]
    for s in range(nz - 1):
        total = total + z_in[s]
    shared[row] = total * factor

    def share(s, c):
        s = far_first(s, row_count)
        pltpu.make_async_remote_copy(
            shared.at[row],
            shared.at[row],
            last_send.at[1],
            last_recv.at[1],
            device_id={"row": row_peer(s)},
            device_id_type=MESH,
        ).start()
        return c

    lax.fori_loop(1, row_count, share, 0)
    spread(last)
    for k in range(blocks):
        grad = total_f[pl.ds(k, fin_dev, stride=f_rows), :]
        fg_ref[:, k * blk : (k + 1) * blk] = grad.astype(BF16)
    got = shared.at[pl.ds(0, row_count - 1)]
    pltpu.make_async_copy(got, got, last_recv.at[1]).wait()
    for k in range(NX):
        wg_ref[k * rows_x : (k + 1) * rows_x, :] = jnp.concatenate(
            [shared[t * NX + k] for t in range(ny)], axis=1
        )

    sent = agg.at[:, pl.ds(0, col_count - 1)]
    pltpu.make_async_copy(sent, sent, fwd_send).wait()
    sent = ga.at[:, pl.ds(0, col_count - 1)]
    pltpu.make_async_copy(sent, sent, bwd_send).wait()
    for g in range(chunks):
        to_core(g).wait_send()
        left_x = first_x_in if g == 0 else x_in.at[g]
        left_y = first_y_in if g == 0 else y_in.at[g]
        pltpu.make_async_copy(left_x, left_x, red_send.at[1, g]).wait()
        pltpu.make_async_copy(left_y, left_y, red_send.at[2, g]).wait()
    pltpu.make_async_copy(z_in, z_in, last_send.at[0]).wait()
    sent = shared.at[pl.ds(0, row_count - 1)]
    pltpu.make_async_copy(sent, sent, last_send.at[1]).wait()


def write_kernel(wg_ref, fg_ref, wg_out, fg_out, sems):
    first = pltpu.make_async_copy(wg_ref, wg_out, sems.at[0])
    second = pltpu.make_async_copy(fg_ref, fg_out, sems.at[1])
    first.start()
    second.start()
    first.wait()
    second.wait()


def shards(features, adj_values, neighbours, counts, labels, layer_weight, label_embed):
    fin_dev, slab_nodes = features.shape
    blocks, slots, blk, _ = adj_values.shape
    fin, fout = layer_weight.shape
    col_count, row_count = lax.axis_size("col"), lax.axis_size("row")
    ny, nz = row_count // NX, col_count // 2
    rows_x, cols_y = fin_dev // NX, fout // ny
    parts = blocks // col_count
    factor = 1.0 / math.sqrt(slab_nodes * row_count)
    in_vmem = pl.BlockSpec(memory_space=pltpu.VMEM)
    in_smem = pl.BlockSpec(memory_space=pltpu.SMEM)
    anywhere = pl.BlockSpec(memory_space=pl.ANY)
    pieces = 4
    zc = 4 if nz % 4 == 0 and nz > 4 else 2
    chunks = nz // zc
    rows_c = zc * rows_x
    f_rows = -(-blocks // 16) * 16
    dma = pltpu.SemaphoreType.DMA

    weight_grad, feature_grad = pl.pallas_call(
        functools.partial(exchange_kernel, col_count, row_count, factor),
        out_shape=(
            jax.ShapeDtypeStruct((fin_dev, fout), F32),
            jax.ShapeDtypeStruct((fin_dev, slab_nodes), BF16),
        ),
        in_specs=[in_smem] * 2 + [in_vmem] * 5 + [anywhere] * 2,
        out_specs=(in_vmem, in_vmem),
        scratch_shapes=[
            pltpu.VMEM((blocks, fin_dev, blk), BF16),
            pltpu.VMEM((parts, col_count, slots * blk, blk), BF16),
            pltpu.VMEM((fin, fout), BF16),
            pltpu.VMEM((parts, col_count, fin_dev, blk), BF16),
            pltpu.VMEM((parts, fin, blk), BF16),
            pltpu.VMEM((parts, blk, fout), BF16),
            pltpu.VMEM((parts, col_count, fin_dev, blk), BF16),
            pltpu.VMEM((parts, col_count, fin_dev, blk), BF16),
            pltpu.VMEM((parts, f_rows, 2 * slots * col_count), BF16),
            pltpu.VMEM((slots * col_count * fin_dev, blk), F32),
            pltpu.VMEM((fin_dev * f_rows, blk), F32),
            pltpu.VMEM((chunks, zc, 2, fin_dev, fout), F32),
            pltpu.VMEM((chunks, zc, fin_dev, fout), BF16),
            pltpu.VMEM((chunks, zc, fin_dev, fout), BF16),
            pltpu.VMEM((chunks, NX, rows_c, fout), BF16),
            pltpu.VMEM((chunks, NX - 1, rows_c, fout), BF16),
            pltpu.VMEM((chunks, ny, rows_c, cols_y), F32),
            pltpu.VMEM((chunks, ny, rows_c, cols_y), BF16),
            pltpu.VMEM((chunks, ny - 1, rows_c, cols_y), BF16),
            pltpu.VMEM((ny, zc * fin_dev, cols_y), BF16),
            pltpu.VMEM((ny - 1, zc * fin_dev, cols_y), BF16),
            pltpu.VMEM((NX, rows_c, cols_y), F32),
            pltpu.VMEM((NX, rows_c, cols_y), BF16),
            pltpu.VMEM((NX - 1, rows_c, cols_y), BF16),
            pltpu.VMEM((nz, rows_x, cols_y), F32),
            pltpu.VMEM((nz - 1, rows_x, cols_y), F32),
            pltpu.VMEM((row_count, rows_x, cols_y), F32),
            dma((parts, pieces)),
            dma,
            dma,
            dma((parts,)),
            dma,
            dma((parts,)),
            dma((3, chunks)),
            dma((3, chunks)),
            dma((2,)),
            dma((2,)),
        ],
        compiler_params=pltpu.CompilerParams(
            collective_id=0, has_side_effects=True, vmem_limit_bytes=VMEM_LIMIT
        ),
        name="exchange",
    )(
        neighbours.T,
        counts,
        neighbours.T,
        counts.reshape(1, blocks),
        features,
        labels.reshape(blocks, blk),
        label_embed,
        adj_values.reshape(parts, col_count, slots * blk, blk),
        layer_weight,
    )
    return pl.pallas_call(
        write_kernel,
        out_shape=(
            jax.ShapeDtypeStruct((fin_dev, fout), F32),
            jax.ShapeDtypeStruct((fin_dev, slab_nodes), BF16),
        ),
        in_specs=[in_vmem] * 2,
        out_specs=(anywhere, anywhere),
        scratch_shapes=[dma((2,))],
        name="write",
    )(weight_grad, feature_grad)


def solution(mesh):
    return jax.shard_map(
        shards,
        mesh=mesh,
        in_specs=(
            P("col", "row"),
            P("row", None, None, None),
            P("row", None),
            P("row"),
            P("row"),
            P(),
            P(),
        ),
        out_specs=(P("col", None), P("col", "row")),
        check_vma=False,
    )
```
